32 devices in a mesh: row: 4 (over y, x), col: 8 (over z, core).
Axes of the slice: x: 2, y: 2, z: 4, core: 2. Of those that a mesh axis runs over, the one named last changes fastest.
Arguments:
- hidden: bfloat16 [640, 7168], P('col', 'row'), may hold values from -6 to 6
- ln_gain: bfloat16 [7168], P('row'), may hold values from 0.099609375 to 1.8984375
- ln_shift: bfloat16 [7168], P('row'), may hold values from -3 to 3
- qkv_weight: bfloat16 [7168, 12288], P('row', 'col'), may hold values from -0.0625 to 0.0625
- qkv_bias: bfloat16 [12288], P('col'), may hold values from -5.351432 to 5.351432
- out_weight: bfloat16 [4096, 7168], P('row', 'col'), may hold values from -0.09375 to 0.09375
- out_bias: bfloat16 [7168], P('col'), may hold values from -3 to 3
- down_qkv: bfloat16 [64, 7168, 16], P(None, 'row'), may hold values from -0.0625 to 0.0625
- up_qkv: bfloat16 [64, 16, 12288], P(None, None, 'col'), may hold values from -1.5 to 1.5
- down_out: bfloat16 [64, 16, 4096], P(None, None, 'col'), may hold values from -0.09375 to 0.09375
- up_out: bfloat16 [64, 16, 7168], P(None, None, 'col'), may hold values from -1.5 to 1.5
- prompt_lens: int32 [4], replicated, may hold values from 1 to 80, as said below
- suffix_lens: int32 [4, 16], replicated, may hold values from 1 to 5, as said below
- group_sizes: int32 [4], replicated, may hold values from 8 to 16, as said below
- group_adapter_choice: int32 [4], replicated, may hold values from 0 to 15
- chosen: int32 [16], replicated, may hold values from 0 to 63, as said below
Outputs:
- attn_out: bfloat16 [640, 7168], P('row', 'col')
The draws below stay inside these ranges and needn't reach their ends.
Inputs may be any that keep to these rules, and one draw needn't show every extreme that they name: `prompt_lens`: one group, drawn from the seed, has a prompt of exactly 80 tokens, 16 requests and every suffix 5 long, so it fills all 160 slots. `suffix_lens`: entries past a group's number of requests are not used. `group_sizes`: A group's prompt and its live suffixes take at most 160 slots. `chosen`: 16 different bank indices.
All inputs are finite; a program needn't handle non-finite values.
Results may differ from the reference program's by a relative error of at most 0.012.
The reference program's roundings to bfloat16 on the way count: a program that leaves them out, or rounds other values in their place, can miss the bound.
Values may be sent and summed in bfloat16 or wider, within the bound.
A program may use at most 128 MiB of HBM per device.

```python
import jax
import jax.numpy as jnp
from jax import lax

D = 7168
HEADS = 32
HEAD_SIZE = 128
RANK = 16
ADAPTER_COUNT = 64
CHOSEN_ADAPTERS = 16
RMAX = 16
GCAP = 160
HD = 4096
REQUEST_GROUPS = 4
TOKENS = 640
S_MAX = 5
P_MAX = 80
WIN = 53


def busiest_group(key):
    return jax.random.randint(jax.random.fold_in(key, 9001), (), 0, REQUEST_GROUPS)


def draw_prompt_lens(key, part):
    busiest = busiest_group(key)
    sampled = jax.random.randint(jax.random.fold_in(key, 11), (REQUEST_GROUPS,), 1, P_MAX + 1)
    return jnp.where(jnp.arange(REQUEST_GROUPS) == busiest, P_MAX, sampled).astype(jnp.int32)


def draw_suffix_lens(key, part):
    busiest = busiest_group(key)
    sampled = jax.random.randint(jax.random.fold_in(key, 12), (REQUEST_GROUPS, RMAX), 1, S_MAX + 1)
    return jnp.where((jnp.arange(REQUEST_GROUPS) == busiest)[:, None], S_MAX, sampled).astype(jnp.int32)


def draw_group_sizes(key, part):
    busiest = busiest_group(key)
    sampled = jax.random.randint(jax.random.fold_in(key, 13), (REQUEST_GROUPS,), RMAX // 2, RMAX + 1)
    return jnp.where(jnp.arange(REQUEST_GROUPS) == busiest, RMAX, sampled).astype(jnp.int32)


def draw_chosen(key, part):
    return jax.random.permutation(jax.random.fold_in(key, 14), ADAPTER_COUNT)[:CHOSEN_ADAPTERS].astype(jnp.int32)


def draw_qkv_bias(key, part):
    base_key = jax.random.fold_in(key, 21)
    sign_key = jax.random.fold_in(key, 22)
    level_key = jax.random.fold_in(key, 23)
    pick_key = jax.random.fold_in(key, 24)
    place_key = jax.random.fold_in(key, 25)
    base = jnp.clip(0.5 * jax.random.normal(base_key, (HEADS, 3, HEAD_SIZE), jnp.float32), -3.0, 3.0)
    top_level = 15.0
    signs = jax.random.rademacher(sign_key, (HEADS, HEAD_SIZE)).astype(jnp.float32)
    drawn_levels = 11.0 + (top_level - 11.0) * jax.random.uniform(level_key, (HEADS,), jnp.float32)
    aligned_flag = jax.random.bernoulli(pick_key, 0.5, (HEADS,))
    forced = jax.random.randint(place_key, (), 0, HEADS)
    head_ids = jnp.arange(HEADS)
    level = jnp.where(aligned_flag, drawn_levels, 0.0)
    level = jnp.where(head_ids == (forced + 1) % HEADS, top_level, level)
    level = jnp.where(head_ids == forced, 0.0, level)
    aligned = (level * HEAD_SIZE ** (-0.25))[:, None] * signs
    hot_head = (level > 0.0)[:, None]
    query_part = jnp.where(hot_head, aligned, base[:, 0])
    key_part = jnp.where(hot_head, aligned, base[:, 1])
    stacked = jnp.stack([query_part, key_part, base[:, 2]], axis=1)
    return stacked.reshape(3 * HEADS * HEAD_SIZE).astype(jnp.bfloat16)


def touch_ends(array, own_key, smallest, top_value):
    dims = array.shape
    index_at = [jax.random.randint(jax.random.fold_in(own_key, axis), (), 0, dims[axis]) for axis in range(len(dims))]
    array = array.at[tuple(index_at)].set(smallest)
    longest = dims.index(max(dims))
    index_at[longest] = (index_at[longest] + 1) % dims[longest]
    return array.at[tuple(index_at)].set(top_value)


def block_scale(key, dims, cuts, smallest, largest):
    def one(axis_at, shards_of):
        draws = jax.random.uniform(jax.random.fold_in(jax.random.fold_in(key, 6), axis_at), (shards_of,), jnp.float32, smallest / len(cuts), largest / len(cuts))
        return jnp.repeat(jnp.exp(draws), dims[axis_at] // shards_of).reshape((-1,) + (1,) * (len(dims) - axis_at - 1))

    level = one(*cuts[0])
    for cut in cuts[1:]:
        level = level * one(*cut)
    return level


def gaussian(rng, dims, deviation, limit, cuts=(), held_as=jnp.bfloat16):
    loudness = block_scale(rng, dims, cuts, -0.22, 0.18) if cuts else 1.0
    array = jax.random.normal(rng, dims, jnp.float32) * deviation * loudness
    return jnp.minimum(jnp.maximum(array, -limit), limit).astype(held_as)


def setup_inputs(seed: int = 0) -> dict:
    seeds = jax.random.split(jax.random.key(seed), 17)
    hidden = gaussian(seeds[0], (TOKENS, D), 1.0, 6.0, ((0, 8), (1, 4)))
    ln_gain = jnp.clip(1.0 + 0.18 * jax.random.normal(seeds[1], (D,), jnp.float32), 0.099609375, 1.8984375).astype(jnp.bfloat16)
    ln_shift = gaussian(seeds[2], (D,), 0.5, 3.0, ((0, 4),))
    qkv_weight = gaussian(seeds[3], (D, 3 * HD), D ** -0.5, 0.0625, ((0, 4), (1, 8)))
    qkv_bias = draw_qkv_bias(jax.random.fold_in(seeds[16], 71), 0)
    out_weight = gaussian(seeds[5], (HD, D), HD ** -0.5, 0.09375, ((0, 4), (1, 8)))
    out_bias = gaussian(seeds[6], (D,), 0.5, 3.0, ((0, 8),))
    down_qkv = gaussian(seeds[7], (ADAPTER_COUNT, D, RANK), D ** -0.5, 0.0625, ((1, 4),))
    up_qkv = gaussian(seeds[8], (ADAPTER_COUNT, RANK, 3 * HD), RANK ** -0.5, 1.5, ((2, 8),))
    down_out = gaussian(seeds[9], (ADAPTER_COUNT, RANK, HD), HD ** -0.5, 0.09375, ((2, 8),))
    up_out = gaussian(seeds[10], (ADAPTER_COUNT, RANK, D), RANK ** -0.5, 1.5, ((2, 8),))
    prompt_lens = draw_prompt_lens(jax.random.fold_in(seeds[16], 71), 0)
    suffix_lens = draw_suffix_lens(jax.random.fold_in(seeds[16], 71), 0)
    group_sizes = draw_group_sizes(jax.random.fold_in(seeds[16], 71), 0)
    group_adapter_choice = touch_ends(jax.random.randint(seeds[14], (REQUEST_GROUPS,), 0, CHOSEN_ADAPTERS), jax.random.fold_in(seeds[14], 1), 0, CHOSEN_ADAPTERS - 1).astype(jnp.int32)
    chosen = draw_chosen(jax.random.fold_in(seeds[16], 71), 0)
    return dict(hidden=hidden, ln_gain=ln_gain, ln_shift=ln_shift, qkv_weight=qkv_weight, qkv_bias=qkv_bias, out_weight=out_weight, out_bias=out_bias, down_qkv=down_qkv, up_qkv=up_qkv, down_out=down_out, up_out=up_out, prompt_lens=prompt_lens, suffix_lens=suffix_lens, group_sizes=group_sizes, group_adapter_choice=group_adapter_choice, chosen=chosen)


def group_layout(prompt, count, suffix):
    offsets = jnp.arange(GCAP, dtype=jnp.int32)
    chosen_adapter_index = jnp.arange(suffix.shape[0], dtype=jnp.int32)
    live_lens = jnp.where(chosen_adapter_index < count, suffix, 0).astype(jnp.int32)
    end_at = (prompt + jnp.cumsum(live_lens)).astype(jnp.int32)
    group_start_rows = end_at - live_lens
    request = lax.optimization_barrier(jnp.sum((offsets[:, None] >= end_at[None, :]).astype(jnp.int32), axis=1))
    in_prompt = offsets < prompt
    live_rows = in_prompt | (request < count)
    group_begin_row = lax.optimization_barrier(jnp.sum(jnp.where(chosen_adapter_index[None, :] == request[:, None], group_start_rows[None, :], 0), axis=1)).astype(jnp.int32)
    position = jnp.where(in_prompt, offsets, prompt + offsets - group_begin_row).astype(jnp.int32)
    request_of = jnp.where(in_prompt, -1, request).astype(jnp.int32)
    return (live_rows, request_of, position)

def key_mask(live_rows, request_of, position):
    shared = (request_of[None, :] == -1) | (request_of[None, :] == request_of[:, None])
    causal = position[None, :] <= position[:, None]
    within = (position[:, None] - position[None, :] < WIN) | (position[None, :] == 0)
    allowed = live_rows[:, None] & live_rows[None, :] & shared & causal & within
    first_key = jnp.arange(GCAP)[None, :] == 0
    return jnp.where(live_rows[:, None], allowed, first_key)

def attention(queries, key_rows, value_rows, allowed):
    scores = jnp.einsum('qhe,khe->hqk', queries.astype(jnp.float32), key_rows.astype(jnp.float32))
    scores = jnp.where(allowed[None], scores, -1e+30)
    highest = lax.optimization_barrier(jnp.max(scores, axis=2, keepdims=True))
    weights = jnp.where(allowed[None], jnp.exp(scores - highest), 0.0)
    probs = (weights / lax.optimization_barrier(jnp.sum(weights, axis=2, keepdims=True))).astype(jnp.bfloat16)
    mixed_rows = jnp.einsum('hqk,khe->qhe', probs.astype(jnp.float32), value_rows.astype(jnp.float32))
    return mixed_rows.astype(jnp.bfloat16).reshape(queries.shape[0], -1)

def reference(hidden, ln_gain, ln_shift, qkv_weight, qkv_bias, out_weight, out_bias, down_qkv, up_qkv, down_out, up_out, prompt_lens, suffix_lens, group_sizes, group_adapter_choice, chosen):
    widened = hidden.astype(jnp.float32)
    average = lax.optimization_barrier(jnp.mean(widened, axis=1, keepdims=True))
    centred = widened - average
    spread = lax.optimization_barrier(jnp.mean(centred * centred, axis=1, keepdims=True))
    normed = (centred * lax.rsqrt(spread + 1e-05) * ln_gain.astype(jnp.float32) + ln_shift.astype(jnp.float32)).astype(jnp.bfloat16)
    adapters = chosen[group_adapter_choice]
    blocks = []
    for group_number in range(REQUEST_GROUPS):
        group_rows = normed[group_number * GCAP:(group_number + 1) * GCAP]
        own_adapter = adapters[group_number]
        projected = jnp.dot(group_rows, qkv_weight, preferred_element_type=jnp.float32)
        reduced = jnp.dot(group_rows, down_qkv[own_adapter], preferred_element_type=jnp.float32).astype(jnp.bfloat16)
        projected = projected + qkv_bias.astype(jnp.float32) + jnp.dot(reduced, up_qkv[own_adapter], preferred_element_type=jnp.float32)
        shaped = projected.reshape(GCAP, HEADS, 3, HEAD_SIZE)
        queries = (shaped[:, :, 0] * HEAD_SIZE ** (-0.5)).astype(jnp.bfloat16)
        key_rows = shaped[:, :, 1].astype(jnp.bfloat16)
        value_rows = shaped[:, :, 2].astype(jnp.bfloat16)
        live_rows, request_of, position = group_layout(prompt_lens[group_number], group_sizes[group_number], suffix_lens[group_number])
        mixed_rows = attention(queries, key_rows, value_rows, key_mask(live_rows, request_of, position))
        reduced_out = jnp.dot(mixed_rows, down_out[own_adapter].T, preferred_element_type=jnp.float32).astype(jnp.bfloat16)
        result = jnp.dot(mixed_rows, out_weight, preferred_element_type=jnp.float32) + out_bias.astype(jnp.float32)
        result = result + jnp.dot(reduced_out, up_out[own_adapter], preferred_element_type=jnp.float32)
        blocks.append((result * live_rows[:, None].astype(jnp.float32)).astype(jnp.bfloat16))
    return jnp.concatenate(blocks, axis=0)
```

```python
import jax
import jax.numpy as jnp
from jax import lax
from jax.sharding import PartitionSpec as P

HEAD_SIZE = 128
GCAP = 160
WIN = 53


def group_layout(prompt, count, suffix):
    offsets = jnp.arange(GCAP, dtype=jnp.int32)
    chosen_adapter_index = jnp.arange(suffix.shape[0], dtype=jnp.int32)
    live_lens = jnp.where(chosen_adapter_index < count, suffix, 0)
    end_at = prompt + jnp.cumsum(live_lens)
    group_start_rows = end_at - live_lens
    request = jnp.sum((offsets[:, None] >= end_at[None, :]).astype(jnp.int32), axis=1)
    in_prompt = offsets < prompt
    live_rows = in_prompt | (request < count)
    group_begin_row = jnp.sum(
        jnp.where(chosen_adapter_index[None, :] == request[:, None], group_start_rows[None, :], 0),
        axis=1,
    )
    position = jnp.where(in_prompt, offsets, prompt + offsets - group_begin_row)
    request_of = jnp.where(in_prompt, -1, request)
    return (live_rows, request_of, position)


def key_mask(live_rows, request_of, position):
    shared = (request_of[None, :] == -1) | (request_of[None, :] == request_of[:, None])
    causal = position[None, :] <= position[:, None]
    within = (position[:, None] - position[None, :] < WIN) | (position[None, :] == 0)
    allowed = live_rows[:, None] & live_rows[None, :] & shared & causal & within
    first_key = jnp.arange(GCAP)[None, :] == 0
    return jnp.where(live_rows[:, None], allowed, first_key)


def attention(queries, key_rows, value_rows, allowed):
    scores = jnp.einsum("qhe,khe->hqk", queries, key_rows, preferred_element_type=jnp.float32)
    scores = jnp.where(allowed[None], scores, -1e30)
    highest = jnp.max(scores, axis=2, keepdims=True)
    weights = jnp.where(allowed[None], jnp.exp(scores - highest), 0.0)
    probs = (weights / jnp.sum(weights, axis=2, keepdims=True)).astype(jnp.bfloat16)
    mixed_rows = jnp.einsum("hqk,khe->qhe", probs, value_rows, preferred_element_type=jnp.float32)
    return mixed_rows.astype(jnp.bfloat16).reshape(queries.shape[0], -1)


def normalise(hidden, ln_gain, ln_shift):
    widened = hidden.astype(jnp.float32)
    width = widened.shape[1]
    own_mean = jnp.mean(widened, axis=1, keepdims=True)
    centred = widened - own_mean
    own_spread = jnp.sum(centred * centred, axis=1, keepdims=True)
    every = lax.all_gather(jnp.concatenate([own_mean, own_spread], axis=1), "row", axis=0)
    means, spreads = every[:, :, :1], every[:, :, 1:]
    average = jnp.mean(means, axis=0)
    between = jnp.sum((means - average) * (means - average), axis=0) * width
    spread = (jnp.sum(spreads, axis=0) + between) / (width * every.shape[0])
    return (
        (widened - average) * lax.rsqrt(spread + 1e-05) * ln_gain.astype(jnp.float32)
        + ln_shift.astype(jnp.float32)
    ).astype(jnp.bfloat16)


def sum_over_row(partial):
    moved = lax.all_to_all(partial, "row", split_axis=0, concat_axis=0, tiled=True)
    blocks = moved.reshape((lax.axis_size("row"), -1) + moved.shape[1:])
    return jnp.sum(blocks.astype(jnp.float32), axis=0)


def local(
    hidden,
    ln_gain,
    ln_shift,
    qkv_weight,
    qkv_bias,
    out_weight,
    out_bias,
    down_qkv,
    up_qkv,
    down_out,
    up_out,
    prompt_lens,
    suffix_lens,
    group_sizes,
    group_adapter_choice,
    chosen,
):
    row_index = lax.axis_index("row")
    groups = lax.axis_size("row")
    adapters = chosen[group_adapter_choice]
    own_adapter = adapters[row_index]
    normed = normalise(hidden, ln_gain, ln_shift)
    tokens = lax.all_gather(normed, "col", axis=0, tiled=True)
    low_part = jnp.einsum(
        "gtd,gdr->gtr",
        tokens.reshape(groups, GCAP, -1),
        down_qkv[adapters],
        preferred_element_type=jnp.float32,
    )
    low = sum_over_row(low_part.reshape(groups * GCAP, -1)).astype(jnp.bfloat16)
    part = jnp.dot(tokens, qkv_weight, preferred_element_type=jnp.float32).astype(jnp.bfloat16)
    projected = (
        sum_over_row(part)
        + qkv_bias.astype(jnp.float32)
        + jnp.dot(low, up_qkv[own_adapter], preferred_element_type=jnp.float32)
    )
    heads_here = projected.shape[1] // (3 * HEAD_SIZE)
    shaped = projected.reshape(GCAP, heads_here, 3, HEAD_SIZE)
    queries = (shaped[:, :, 0] * HEAD_SIZE ** (-0.5)).astype(jnp.bfloat16)
    key_rows = shaped[:, :, 1].astype(jnp.bfloat16)
    value_rows = shaped[:, :, 2].astype(jnp.bfloat16)
    live_rows, request_of, position = group_layout(
        prompt_lens[row_index], group_sizes[row_index], suffix_lens[row_index]
    )
    mixed_rows = attention(queries, key_rows, value_rows, key_mask(live_rows, request_of, position))
    all_heads = lax.all_gather(mixed_rows, "col", axis=1, tiled=True)
    down_full = lax.all_gather(down_out[own_adapter], "col", axis=1, tiled=True)
    reduced_out = lax.dot_general(
        all_heads, down_full, (((1,), (1,)), ((), ())), preferred_element_type=jnp.float32
    ).astype(jnp.bfloat16)
    gathered = lax.all_to_all(all_heads, "row", split_axis=1, concat_axis=0, tiled=True)
    out_part = jnp.dot(gathered, out_weight, preferred_element_type=jnp.float32)
    result = (
        sum_over_row(out_part.astype(jnp.bfloat16))
        + out_bias.astype(jnp.float32)
        + jnp.dot(reduced_out, up_out[own_adapter], preferred_element_type=jnp.float32)
    )
    return (result * live_rows[:, None].astype(jnp.float32)).astype(jnp.bfloat16)


def solution(mesh):
    in_specs = (
        P("col", "row"),
        P("row"),
        P("row"),
        P("row", "col"),
        P("col"),
        P("row", "col"),
        P("col"),
        P(None, "row", None),
        P(None, None, "col"),
        P(None, None, "col"),
        P(None, None, "col"),
        P(),
        P(),
        P(),
        P(),
        P(),
    )
    out_specs = P("row", "col")
    return jax.shard_map(local, mesh=mesh, in_specs=in_specs, out_specs=out_specs, check_vma=False)
```

```python
import functools

import jax
import jax.numpy as jnp
from jax import lax
from jax.experimental import pallas as pl
from jax.experimental.pallas import tpu as pltpu
from jax.sharding import PartitionSpec as P

HEAD_SIZE = 128
GCAP = 160
WIN = 53


def group_layout(prompt, count, suffix):
    offsets = jnp.arange(GCAP, dtype=jnp.int32)
    chosen_adapter_index = jnp.arange(suffix.shape[0], dtype=jnp.int32)
    live_lens = jnp.where(chosen_adapter_index < count, suffix, 0)
    end_at = prompt + jnp.cumsum(live_lens)
    group_start_rows = end_at - live_lens
    request = jnp.sum((offsets[:, None] >= end_at[None, :]).astype(jnp.int32), axis=1)
    in_prompt = offsets < prompt
    live_rows = in_prompt | (request < count)
    group_begin_row = jnp.sum(
        jnp.where(chosen_adapter_index[None, :] == request[:, None], group_start_rows[None, :], 0),
        axis=1,
    )
    position = jnp.where(in_prompt, offsets, prompt + offsets - group_begin_row)
    request_of = jnp.where(in_prompt, -1, request)
    return (live_rows, request_of, position)


def key_mask(live_rows, request_of, position):
    shared = (request_of[None, :] == -1) | (request_of[None, :] == request_of[:, None])
    causal = position[None, :] <= position[:, None]
    within = (position[:, None] - position[None, :] < WIN) | (position[None, :] == 0)
    allowed = live_rows[:, None] & live_rows[None, :] & shared & causal & within
    first_key = jnp.arange(GCAP)[None, :] == 0
    return jnp.where(live_rows[:, None], allowed, first_key)


def attention(queries, key_rows, value_rows, allowed):
    scores = jnp.einsum("qhe,khe->hqk", queries, key_rows, preferred_element_type=jnp.float32)
    scores = jnp.where(allowed[None], scores, -1e30)
    highest = jnp.max(scores, axis=2, keepdims=True)
    weights = jnp.where(allowed[None], jnp.exp(scores - highest), 0.0)
    probs = (weights / jnp.sum(weights, axis=2, keepdims=True)).astype(jnp.bfloat16)
    mixed_rows = jnp.einsum("hqk,khe->qhe", probs, value_rows, preferred_element_type=jnp.float32)
    return mixed_rows.astype(jnp.bfloat16).reshape(queries.shape[0], -1)


def normalise(hidden, ln_gain, ln_shift):
    widened = hidden.astype(jnp.float32)
    width = widened.shape[1]
    own_mean = jnp.mean(widened, axis=1, keepdims=True)
    centred = widened - own_mean
    own_spread = jnp.sum(centred * centred, axis=1, keepdims=True)
    every = lax.all_gather(jnp.concatenate([own_mean, own_spread], axis=1), "row", axis=0)
    means, spreads = every[:, :, :1], every[:, :, 1:]
    average = jnp.mean(means, axis=0)
    between = jnp.sum((means - average) * (means - average), axis=0) * width
    spread = (jnp.sum(spreads, axis=0) + between) / (width * every.shape[0])
    return (
        (widened - average) * lax.rsqrt(spread + 1e-05) * ln_gain.astype(jnp.float32)
        + ln_shift.astype(jnp.float32)
    ).astype(jnp.bfloat16)


def sum_over_row(partial):
    moved = lax.all_to_all(partial, "row", split_axis=0, concat_axis=0, tiled=True)
    blocks = moved.reshape((lax.axis_size("row"), -1) + moved.shape[1:])
    return jnp.sum(blocks.astype(jnp.float32), axis=0)


def local(
    hidden,
    ln_gain,
    ln_shift,
    qkv_weight,
    qkv_bias,
    out_weight,
    out_bias,
    down_qkv,
    up_qkv,
    down_out,
    up_out,
    prompt_lens,
    suffix_lens,
    group_sizes,
    group_adapter_choice,
    chosen,
):
    row_index = lax.axis_index("row")
    groups = lax.axis_size("row")
    adapters = chosen[group_adapter_choice]
    own_adapter = adapters[row_index]
    normed = normalise(hidden, ln_gain, ln_shift)
    tokens = lax.all_gather(normed, "col", axis=0, tiled=True)
    low_part = jnp.einsum(
        "gtd,gdr->gtr",
        tokens.reshape(groups, GCAP, -1),
        down_qkv[adapters],
        preferred_element_type=jnp.float32,
    )
    low = sum_over_row(low_part.reshape(groups * GCAP, -1)).astype(jnp.bfloat16)
    part = jnp.dot(tokens, qkv_weight, preferred_element_type=jnp.float32).astype(jnp.bfloat16)
    projected = (
        sum_over_row(part)
        + qkv_bias.astype(jnp.float32)
        + jnp.dot(low, up_qkv[own_adapter], preferred_element_type=jnp.float32)
    )
    heads_here = projected.shape[1] // (3 * HEAD_SIZE)
    shaped = projected.reshape(GCAP, heads_here, 3, HEAD_SIZE)
    queries = (shaped[:, :, 0] * HEAD_SIZE ** (-0.5)).astype(jnp.bfloat16)
    key_rows = shaped[:, :, 1].astype(jnp.bfloat16)
    value_rows = shaped[:, :, 2].astype(jnp.bfloat16)
    live_rows, request_of, position = group_layout(
        prompt_lens[row_index], group_sizes[row_index], suffix_lens[row_index]
    )
    mixed_rows = attention(queries, key_rows, value_rows, key_mask(live_rows, request_of, position))
    all_heads = lax.all_gather(mixed_rows, "col", axis=1, tiled=True)
    down_full = lax.all_gather(down_out[own_adapter], "col", axis=1, tiled=True)
    reduced_out = lax.dot_general(
        all_heads, down_full, (((1,), (1,)), ((), ())), preferred_element_type=jnp.float32
    ).astype(jnp.bfloat16)
    gathered = lax.all_to_all(all_heads, "row", split_axis=1, concat_axis=0, tiled=True)
    out_part = jnp.dot(gathered, out_weight, preferred_element_type=jnp.float32)
    result = (
        sum_over_row(out_part.astype(jnp.bfloat16))
        + out_bias.astype(jnp.float32)
        + jnp.dot(reduced_out, up_out[own_adapter], preferred_element_type=jnp.float32)
    )
    return (result * live_rows[:, None].astype(jnp.float32)).astype(jnp.bfloat16)


HIDDEN_PART = 3 * HEAD_SIZE
BF = jnp.bfloat16
F32 = jnp.float32


def fused_kernel(
    planes,
    hidden,
    gain,
    shift,
    qkv_bias,
    out_bias,
    prompt_lens,
    suffix_lens,
    group_sizes,
    choice,
    chosen,
    qkv_hbm,
    out_hbm,
    down_qkv_hbm,
    up_qkv_hbm,
    down_out_hbm,
    up_out_hbm,
    out,
    qkv_w,
    out_w,
    down_qkv,
    up_qkv,
    down_out,
    up_out,
    stats,
    x,
    part_out,
    part_in,
    part_own,
    low_own,
    low_in,
    mixed_out,
    mixed,
    res_out,
    res_in,
    res_own,
    lowo_out,
    lowo_in,
    lowo_own,
    load_sem,
    stat_send,
    stat_recv,
    x_send,
    x_recv,
    part_send,
    part_recv,
    low_send,
    low_recv,
    mixed_send,
    mixed_recv,
    chain_send,
    chain_recv,
    res_send,
    res_recv,
    lowo_send,
    lowo_recv,
):
    rows = planes
    r = lax.axis_index("row")
    c = lax.axis_index("col")
    z = c // 2
    k = c % 2
    sib = c + 1 - 2 * k
    block = hidden.shape[0]
    head_col = pl.multiple_of(r * HIDDEN_PART, 128)

    def to(src, dst, send, recv, row, col):
        return pltpu.make_async_remote_copy(
            src_ref=src,
            dst_ref=dst,
            send_sem=send,
            recv_sem=recv,
            device_id=(row, col),
            device_id_type=pl.DeviceIdType.MESH,
        )

    loads = [
        pltpu.make_async_copy(qkv_hbm, qkv_w, load_sem.at[0]),
        pltpu.make_async_copy(down_qkv_hbm, down_qkv, load_sem.at[1]),
        pltpu.make_async_copy(
            up_qkv_hbm.at[:, :, pl.ds(head_col, HIDDEN_PART)], up_qkv, load_sem.at[2]
        ),
        pltpu.make_async_copy(down_out_hbm, down_out, load_sem.at[3]),
        pltpu.make_async_copy(out_hbm, out_w, load_sem.at[4]),
        pltpu.make_async_copy(up_out_hbm, up_out, load_sem.at[5]),
    ]
    for load in loads:
        load.start()

    barrier = pltpu.get_barrier_semaphore()

    def greet(row, col):
        pl.semaphore_signal(
            barrier, inc=1, device_id=(row, col), device_id_type=pl.DeviceIdType.MESH
        )

    greet(r, sib)
    for step in range(1, rows):
        greet((r + step) % rows, c)

    @pl.when(z > 0)
    def _():
        greet(r, c - 2)

    @pl.when(z < planes - 1)
    def _():
        greet(r, c + 2)

    before = (z + planes - 1) // planes
    after = (2 * planes - 2 - z) // planes
    pl.semaphore_wait(barrier, rows + before + after)

    wide = hidden[...].astype(F32)
    width = wide.shape[1]
    own_mean = jnp.mean(wide, axis=1, keepdims=True)
    centred = wide - own_mean
    own_spread = jnp.sum(centred * centred, axis=1, keepdims=True)
    lane = lax.broadcasted_iota(jnp.int32, (block, 128), 1)
    stats[r] = jnp.where(lane == 0, own_mean, own_spread)

    def stat_copy(row):
        return to(stats.at[r], stats.at[r], stat_send.at[row], stat_recv.at[r], row, c)

    for step in range(1, rows):
        stat_copy((r + step) % rows).start()
    for step in range(1, rows):
        peer = (r + step) % rows
        to(stats.at[peer], stats.at[peer], stat_send.at[peer], stat_recv.at[peer], r, c).wait_recv()
    means = [stats[i][:, 0:1] for i in range(rows)]
    average = sum(means) / rows
    spread = sum(stats[i][:, 1:2] for i in range(rows))
    spread = spread + width * sum((m - average) * (m - average) for m in means)
    spread = spread / (width * rows)

    def x_rows(index):
        return pl.ds(pl.multiple_of(index * block, 16), block)

    x[x_rows(c), :] = (
        (hidden[...].astype(F32) - average)
        * lax.rsqrt(spread + 1e-05)
        * gain[...].astype(F32)
        + shift[...].astype(F32)
    ).astype(BF)

    def x_copy(way, group, col):
        at = x_rows(2 * group + k)
        return to(
            x.at[at], x.at[at], x_send.at[way, group], x_recv.at[2 * group + k], r, col
        )

    def x_wait(index):
        at = x_rows(index)
        to(x.at[at], x.at[at], x_send.at[0, 0], x_recv.at[index], r, c).wait_recv()

    def part_copy(group, row):
        return to(
            part_out.at[group, row],
            part_in.at[group, r],
            part_send.at[group, row],
            part_recv.at[group, r],
            row,
            c,
        )

    def low_copy(group, row):
        return to(
            low_own.at[group],
            low_in.at[group, r],
            low_send.at[group, row],
            low_recv.at[group, r],
            row,
            c,
        )

    def adapter(group):
        return chosen[choice[group]]

    def token_rows(group):
        return pl.ds(pl.multiple_of(group * GCAP, 16), GCAP)

    def project(group):
        low_own[group] = lax.dot_general(
            down_qkv[adapter(group)],
            x[token_rows(group), :],
            (((1,), (1,)), ((), ())),
            preferred_element_type=F32,
        )
        for step in range(1, rows):
            low_copy(group, (r + step) % rows).start()

        def one(step, _):
            row = (r + step) % rows
            cols = pl.ds(pl.multiple_of(row * HIDDEN_PART, 128), HIDDEN_PART)
            part = jnp.dot(
                x[token_rows(group), :], qkv_w[:, cols], preferred_element_type=F32
            )

            @pl.when(row != r)
            def _():
                part_out[group, row] = part.astype(BF)
                part_copy(group, row).start()

            @pl.when(row == r)
            def _():
                part_own[group] = part

            return 0

        lax.fori_loop(1, rows + 1, one, 0)

    def layout(group, axis):
        shape = (GCAP, 1) if axis == 0 else (1, GCAP)
        offsets = lax.broadcasted_iota(jnp.int32, shape, axis)
        prompt = prompt_lens[group]
        count = group_sizes[group]
        end = prompt
        request = jnp.zeros(shape, jnp.int32)
        begin = jnp.zeros(shape, jnp.int32)
        for j in range(suffix_lens.shape[1]):
            start = end
            end = end + jnp.where(j < count, suffix_lens[group, j], 0)
            passed = jnp.where(offsets >= end, 1, 0)
            begin = begin + jnp.where(offsets >= start, (1 - passed) * start, 0)
            request = request + passed
        inside = offsets < prompt
        position = jnp.where(inside, offsets, prompt + offsets - begin)
        request = jnp.where(inside, -1, jnp.where(request < count, request, -2))
        return offsets, request, position

    def allowed_of(group):
        _, request_q, position_q = layout(group, 0)
        key, request_k, position_k = layout(group, 1)
        square = (GCAP, GCAP)
        rq = jnp.broadcast_to(request_q, square)
        rk = jnp.broadcast_to(request_k, square)
        pq = jnp.broadcast_to(position_q, square)
        pk = jnp.broadcast_to(position_k, square)
        keys = jnp.broadcast_to(key, square)
        shared = (rk == -1) | ((rk == rq) & (rk != -2))
        near = (pq - pk < WIN) | (pk == 0)
        live = shared & (pk <= pq) & near & (rq != -2)
        return live | ((rq == -2) & (keys == 0))

    def mixed_copy(group, row_from):
        return to(
            mixed_out.at[group],
            mixed.at[group, k, pl.ds(0, GCAP), pl.ds(pl.multiple_of(row_from * 128, 128), 128)],
            mixed_send.at[group],
            mixed_recv.at[group, row_from],
            z,
            c,
        )

    def attend(group):
        low = low_own[group]
        proj = part_own[group] + qkv_bias[:, pl.ds(head_col, HIDDEN_PART)].astype(F32)
        for step in range(1, rows):
            peer = (r + step) % rows
            to(
                low_own.at[group], low_in.at[group, peer],
                low_send.at[group, peer], low_recv.at[group, peer], r, c,
            ).wait_recv()
            low = low + low_in[group, peer]
        for step in range(1, rows):
            peer = (r + step) % rows
            to(
                part_out.at[group, peer], part_in.at[group, peer],
                part_send.at[group, peer], part_recv.at[group, peer], r, c,
            ).wait_recv()
            proj = proj + part_in[group, peer].astype(F32)
        proj = proj + lax.dot_general(
            low.astype(BF), up_qkv[adapter(group)], (((0,), (0,)), ((), ())),
            preferred_element_type=F32,
        )
        query = (proj[:, :HEAD_SIZE] * HEAD_SIZE ** (-0.5)).astype(BF)
        key = proj[:, HEAD_SIZE : 2 * HEAD_SIZE].astype(BF)
        value = proj[:, 2 * HEAD_SIZE :].astype(BF)
        allowed = allowed_of(group)
        scores = lax.dot_general(
            query, key, (((1,), (1,)), ((), ())), preferred_element_type=F32
        )
        scores = jnp.where(allowed, scores, -1e30)
        highest = jnp.max(scores, axis=1, keepdims=True)
        weights = jnp.where(allowed, jnp.exp(scores - highest), 0.0)
        probs = (weights / jnp.sum(weights, axis=1, keepdims=True)).astype(BF)
        rows_mixed = jnp.dot(probs, value, preferred_element_type=F32).astype(BF)

        @pl.when(r == z)
        def _():
            mixed[group, k, pl.ds(0, GCAP), pl.ds(pl.multiple_of(r * 128, 128), 128)] = rows_mixed
            mixed[group, k, pl.ds(GCAP, 16), :] = down_out[adapter(group)]

        @pl.when(r != z)
        def _():
            mixed_out[group] = rows_mixed
            mixed_copy(group, r).start()

    loads[0].wait()
    loads[1].wait()
    loads[2].wait()
    loads[3].wait()

    def first(step, _):
        @pl.when(step < planes)
        def _():
            for side in range(2):
                group = z + step * (2 * side - 1)
                valid = (group >= 0) & (group < planes)
                if side == 1:
                    valid = valid & (step > 0)

                @pl.when(valid)
                def _():
                    @pl.when(step > 0)
                    def _():
                        x_wait(2 * group + k)

                    @pl.when((group <= z) & (z < planes - 1))
                    def _():
                        x_copy(0, group, c + 2).start()

                    @pl.when((group >= z) & (z > 0))
                    def _():
                        x_copy(1, group, c - 2).start()

                    x_copy(2, group, sib).start()

            def compute(side, _):
                group = z + step * (2 * side - 1)

                @pl.when((group >= 0) & (group < planes) & (step + 1 - side > 0))
                def _():
                    x_wait(2 * group + 1 - k)
                    project(group)

                return 0

            lax.fori_loop(0, 2, compute, 0)

        @pl.when(step > 0)
        def _():
            def mix(side, _):
                group = z + (step - 1) * (2 * side - 1)

                @pl.when((group >= 0) & (group < planes) & (step - side > 0))
                def _():
                    attend(group)

                return 0

            lax.fori_loop(0, 2, mix, 0)

        return 0

    lax.fori_loop(0, planes + 1, first, 0)
    loads[4].wait()
    loads[5].wait()

    def chain_copy(way, group, col):
        return to(
            mixed.at[group, k], mixed.at[group, k],
            chain_send.at[way, group], chain_recv.at[group, k], r, col,
        )

    def chain_wait(group, half):
        to(
            mixed.at[group, half], mixed.at[group, half],
            chain_send.at[0, group], chain_recv.at[group, half], r, c,
        ).wait_recv()

    def res_copy(group):
        return to(res_out.at[group], res_in.at[r], res_send.at[group], res_recv.at[r], group, c)

    def lowo_copy(group):
        return to(
            lowo_out.at[group], lowo_in.at[r], lowo_send.at[group], lowo_recv.at[r], group, c
        )

    half_rows = out_w.shape[0] // 2

    def combine(group):
        @pl.when(z == r)
        def _():
            for step in range(1, rows):
                mixed_copy(group, (r + step) % rows).wait_recv()

        @pl.when(z != r)
        def _():
            chain_wait(group, k)

        @pl.when((z >= r) & (z < planes - 1))
        def _():
            chain_copy(0, group, c + 2).start()

        @pl.when((z <= r) & (z > 0))
        def _():
            chain_copy(1, group, c - 2).start()

        chain_copy(2, group, sib).start()
        chain_wait(group, 1 - k)
        low = jnp.zeros((16, GCAP), F32)
        part = jnp.zeros((GCAP, out_w.shape[1]), F32)
        for half in range(2):
            tokens = mixed[group, half, pl.ds(0, GCAP), :]
            low = low + lax.dot_general(
                mixed[group, half, pl.ds(GCAP, 16), :], tokens, (((1,), (1,)), ((), ())),
                preferred_element_type=F32,
            )
            part = part + jnp.dot(
                tokens, out_w[half * half_rows : (half + 1) * half_rows, :],
                preferred_element_type=F32,
            )

        @pl.when(group != r)
        def _():
            lowo_out[group] = low
            lowo_copy(group).start()
            res_out[group] = part.astype(BF)
            res_copy(group).start()

        @pl.when(group == r)
        def _():
            lowo_own[...] = low
            res_own[...] = part

    def second(step, _):
        side = step % 2
        group = r + (step // 2) * (2 * side - 1)

        @pl.when((group >= 0) & (group < planes) & (step != 1))
        def _():
            combine(group)

        return 0

    lax.fori_loop(0, 2 * planes, second, 0)

    _, request, _ = layout(r, 0)
    alive = jnp.where(request != -2, 1.0, 0.0)
    low = lowo_own[...]
    total = res_own[...] + out_bias[...].astype(F32)
    for step in range(1, rows):
        peer = (r + step) % rows
        to(
            lowo_out.at[peer], lowo_in.at[peer], lowo_send.at[peer], lowo_recv.at[peer], r, c
        ).wait_recv()
        low = low + lowo_in[peer]
    for step in range(1, rows):
        peer = (r + step) % rows
        to(
            res_out.at[peer], res_in.at[peer], res_send.at[peer], res_recv.at[peer], r, c
        ).wait_recv()
        total = total + res_in[peer].astype(F32)
    total = total + lax.dot_general(
        low.astype(BF), up_out[adapter(r)], (((0,), (0,)), ((), ())), preferred_element_type=F32
    )
    out[...] = (total * alive).astype(BF)

    for step in range(1, rows):
        peer = (r + step) % rows
        stat_copy(peer).wait_send()
        res_copy(peer).wait_send()
        lowo_copy(peer).wait_send()

    def drain(group, _):
        @pl.when((group <= z) & (z < planes - 1))
        def _():
            x_copy(0, group, c + 2).wait_send()

        @pl.when((group >= z) & (z > 0))
        def _():
            x_copy(1, group, c - 2).wait_send()

        x_copy(2, group, sib).wait_send()
        for step in range(1, rows):
            peer = (r + step) % rows
            low_copy(group, peer).wait_send()
            part_copy(group, peer).wait_send()

        @pl.when(r != z)
        def _():
            mixed_copy(group, r).wait_send()

        @pl.when((z >= r) & (z < planes - 1))
        def _():
            chain_copy(0, group, c + 2).wait_send()

        @pl.when((z <= r) & (z > 0))
        def _():
            chain_copy(1, group, c - 2).wait_send()

        chain_copy(2, group, sib).wait_send()
        return 0

    lax.fori_loop(0, planes, drain, 0)


def fused(
    hidden,
    ln_gain,
    ln_shift,
    qkv_weight,
    qkv_bias,
    out_weight,
    out_bias,
    down_qkv,
    up_qkv,
    down_out,
    up_out,
    prompt_lens,
    suffix_lens,
    group_sizes,
    group_adapter_choice,
    chosen,
):
    groups = lax.axis_size("row")
    block, width = hidden.shape
    out_cols = out_weight.shape[1]
    bank, rank = down_out.shape[0], down_out.shape[1]
    down_t = jnp.transpose(down_qkv, (0, 2, 1))
    vmem = pl.BlockSpec(memory_space=pltpu.VMEM)
    smem = pl.BlockSpec(memory_space=pltpu.SMEM)
    hbm = pl.BlockSpec(memory_space=pl.ANY)
    dma = pltpu.SemaphoreType.DMA
    half = HEAD_SIZE * groups
    macs = groups * GCAP * (qkv_weight.size + out_weight.size)
    return pl.pallas_call(
        functools.partial(fused_kernel, groups),
        out_shape=jax.ShapeDtypeStruct((GCAP, out_cols), BF),
        in_specs=[vmem] * 5 + [smem] * 5 + [hbm] * 6,
        out_specs=vmem,
        scratch_shapes=[
            pltpu.VMEM(qkv_weight.shape, BF),
            pltpu.VMEM(out_weight.shape, BF),
            pltpu.VMEM(down_t.shape, BF),
            pltpu.VMEM((bank, rank, HIDDEN_PART), BF),
            pltpu.VMEM(down_out.shape, BF),
            pltpu.VMEM(up_out.shape, BF),
            pltpu.VMEM((groups, block, 128), F32),
            pltpu.VMEM((groups * GCAP, width), BF),
            pltpu.VMEM((groups, groups, GCAP, HIDDEN_PART), BF),
            pltpu.VMEM((groups, groups, GCAP, HIDDEN_PART), BF),
            pltpu.VMEM((groups, GCAP, HIDDEN_PART), F32),
            pltpu.VMEM((groups, rank, GCAP), F32),
            pltpu.VMEM((groups, groups, rank, GCAP), F32),
            pltpu.VMEM((groups, GCAP, HEAD_SIZE), BF),
            pltpu.VMEM((groups, 2, GCAP + rank, half), BF),
            pltpu.VMEM((groups, GCAP, out_cols), BF),
            pltpu.VMEM((groups, GCAP, out_cols), BF),
            pltpu.VMEM((GCAP, out_cols), F32),
            pltpu.VMEM((groups, rank, GCAP), F32),
            pltpu.VMEM((groups, rank, GCAP), F32),
            pltpu.VMEM((rank, GCAP), F32),
            dma((6,)),
            dma((groups,)),
            dma((groups,)),
            dma((3, groups)),
            dma((2 * groups,)),
            dma((groups, groups)),
            dma((groups, groups)),
            dma((groups, groups)),
            dma((groups, groups)),
            dma((groups,)),
            dma((groups, groups)),
            dma((3, groups)),
            dma((groups, 2)),
            dma((groups,)),
            dma((groups,)),
            dma((groups,)),
            dma((groups,)),
        ],
        compiler_params=pltpu.CompilerParams(
            collective_id=0, has_side_effects=True, vmem_limit_bytes=52 * 2**20
        ),
        cost_estimate=pl.CostEstimate(
            flops=2 * macs, bytes_accessed=2 * (qkv_weight.size + out_weight.size), transcendentals=0
        ),
    )(
        hidden,
        ln_gain[None],
        ln_shift[None],
        qkv_bias[None],
        out_bias[None],
        prompt_lens,
        suffix_lens,
        group_sizes,
        group_adapter_choice,
        chosen,
        qkv_weight,
        out_weight,
        down_t,
        up_qkv,
        down_out,
        up_out,
    )


def block_of(*arrays):
    groups = lax.axis_size("row")
    heads_here = arrays[4].shape[0] // HIDDEN_PART
    if heads_here == groups and lax.axis_size("col") == 2 * groups and arrays[5].shape[1] % 128 == 0:
        return fused(*arrays)
    return local(*arrays)


def solution(mesh):
    in_specs = (
        P("col", "row"),
        P("row"),
        P("row"),
        P("row", "col"),
        P("col"),
        P("row", "col"),
        P("col"),
        P(None, "row", None),
        P(None, None, "col"),
        P(None, None, "col"),
        P(None, None, "col"),
        P(),
        P(),
        P(),
        P(),
        P(),
    )
    out_specs = P("row", "col")
    return jax.shard_map(block_of, mesh=mesh, in_specs=in_specs, out_specs=out_specs, check_vma=False)
```

```python
import functools

import jax
import jax.numpy as jnp
from jax import lax
from jax.experimental import pallas as pl
from jax.experimental.pallas import tpu as pltpu
from jax.sharding import PartitionSpec as P

HEAD_SIZE = 128
GCAP = 160
WIN = 53


def group_layout(prompt, count, suffix):
    offsets = jnp.arange(GCAP, dtype=jnp.int32)
    chosen_adapter_index = jnp.arange(suffix.shape[0], dtype=jnp.int32)
    live_lens = jnp.where(chosen_adapter_index < count, suffix, 0)
    end_at = prompt + jnp.cumsum(live_lens)
    group_start_rows = end_at - live_lens
    request = jnp.sum((offsets[:, None] >= end_at[None, :]).astype(jnp.int32), axis=1)
    in_prompt = offsets < prompt
    live_rows = in_prompt | (request < count)
    group_begin_row = jnp.sum(
        jnp.where(chosen_adapter_index[None, :] == request[:, None], group_start_rows[None, :], 0),
        axis=1,
    )
    position = jnp.where(in_prompt, offsets, prompt + offsets - group_begin_row)
    request_of = jnp.where(in_prompt, -1, request)
    return (live_rows, request_of, position)


def key_mask(live_rows, request_of, position):
    shared = (request_of[None, :] == -1) | (request_of[None, :] == request_of[:, None])
    causal = position[None, :] <= position[:, None]
    within = (position[:, None] - position[None, :] < WIN) | (position[None, :] == 0)
    allowed = live_rows[:, None] & live_rows[None, :] & shared & causal & within
    first_key = jnp.arange(GCAP)[None, :] == 0
    return jnp.where(live_rows[:, None], allowed, first_key)


def attention(queries, key_rows, value_rows, allowed):
    scores = jnp.einsum("qhe,khe->hqk", queries, key_rows, preferred_element_type=jnp.float32)
    scores = jnp.where(allowed[None], scores, -1e30)
    highest = jnp.max(scores, axis=2, keepdims=True)
    weights = jnp.where(allowed[None], jnp.exp(scores - highest), 0.0)
    probs = (weights / jnp.sum(weights, axis=2, keepdims=True)).astype(jnp.bfloat16)
    mixed_rows = jnp.einsum("hqk,khe->qhe", probs, value_rows, preferred_element_type=jnp.float32)
    return mixed_rows.astype(jnp.bfloat16).reshape(queries.shape[0], -1)


def normalise(hidden, ln_gain, ln_shift):
    widened = hidden.astype(jnp.float32)
    width = widened.shape[1]
    own_mean = jnp.mean(widened, axis=1, keepdims=True)
    centred = widened - own_mean
    own_spread = jnp.sum(centred * centred, axis=1, keepdims=True)
    every = lax.all_gather(jnp.concatenate([own_mean, own_spread], axis=1), "row", axis=0)
    means, spreads = every[:, :, :1], every[:, :, 1:]
    average = jnp.mean(means, axis=0)
    between = jnp.sum((means - average) * (means - average), axis=0) * width
    spread = (jnp.sum(spreads, axis=0) + between) / (width * every.shape[0])
    return (
        (widened - average) * lax.rsqrt(spread + 1e-05) * ln_gain.astype(jnp.float32)
        + ln_shift.astype(jnp.float32)
    ).astype(jnp.bfloat16)


def sum_over_row(partial):
    moved = lax.all_to_all(partial, "row", split_axis=0, concat_axis=0, tiled=True)
    blocks = moved.reshape((lax.axis_size("row"), -1) + moved.shape[1:])
    return jnp.sum(blocks.astype(jnp.float32), axis=0)


def local(
    hidden,
    ln_gain,
    ln_shift,
    qkv_weight,
    qkv_bias,
    out_weight,
    out_bias,
    down_qkv,
    up_qkv,
    down_out,
    up_out,
    prompt_lens,
    suffix_lens,
    group_sizes,
    group_adapter_choice,
    chosen,
):
    row_index = lax.axis_index("row")
    groups = lax.axis_size("row")
    adapters = chosen[group_adapter_choice]
    own_adapter = adapters[row_index]
    normed = normalise(hidden, ln_gain, ln_shift)
    tokens = lax.all_gather(normed, "col", axis=0, tiled=True)
    low_part = jnp.einsum(
        "gtd,gdr->gtr",
        tokens.reshape(groups, GCAP, -1),
        down_qkv[adapters],
        preferred_element_type=jnp.float32,
    )
    low = sum_over_row(low_part.reshape(groups * GCAP, -1)).astype(jnp.bfloat16)
    part = jnp.dot(tokens, qkv_weight, preferred_element_type=jnp.float32).astype(jnp.bfloat16)
    projected = (
        sum_over_row(part)
        + qkv_bias.astype(jnp.float32)
        + jnp.dot(low, up_qkv[own_adapter], preferred_element_type=jnp.float32)
    )
    heads_here = projected.shape[1] // (3 * HEAD_SIZE)
    shaped = projected.reshape(GCAP, heads_here, 3, HEAD_SIZE)
    queries = (shaped[:, :, 0] * HEAD_SIZE ** (-0.5)).astype(jnp.bfloat16)
    key_rows = shaped[:, :, 1].astype(jnp.bfloat16)
    value_rows = shaped[:, :, 2].astype(jnp.bfloat16)
    live_rows, request_of, position = group_layout(
        prompt_lens[row_index], group_sizes[row_index], suffix_lens[row_index]
    )
    mixed_rows = attention(queries, key_rows, value_rows, key_mask(live_rows, request_of, position))
    all_heads = lax.all_gather(mixed_rows, "col", axis=1, tiled=True)
    down_full = lax.all_gather(down_out[own_adapter], "col", axis=1, tiled=True)
    reduced_out = lax.dot_general(
        all_heads, down_full, (((1,), (1,)), ((), ())), preferred_element_type=jnp.float32
    ).astype(jnp.bfloat16)
    gathered = lax.all_to_all(all_heads, "row", split_axis=1, concat_axis=0, tiled=True)
    out_part = jnp.dot(gathered, out_weight, preferred_element_type=jnp.float32)
    result = (
        sum_over_row(out_part.astype(jnp.bfloat16))
        + out_bias.astype(jnp.float32)
        + jnp.dot(reduced_out, up_out[own_adapter], preferred_element_type=jnp.float32)
    )
    return (result * live_rows[:, None].astype(jnp.float32)).astype(jnp.bfloat16)


HIDDEN_PART = 3 * HEAD_SIZE
BF = jnp.bfloat16
F32 = jnp.float32


def fused_kernel(
    planes,
    hidden_hbm,
    gain_hbm,
    shift_hbm,
    qkv_bias_hbm,
    out_bias_hbm,
    prompt_lens_hbm,
    suffix_lens_hbm,
    group_sizes_hbm,
    choice_hbm,
    chosen_hbm,
    qkv_hbm,
    out_hbm,
    down_qkv_hbm,
    up_qkv_hbm,
    down_out_hbm,
    up_out_hbm,
    out,
    hidden,
    gain,
    shift,
    qkv_bias,
    out_bias,
    prompt_lens,
    suffix_lens,
    group_sizes,
    choice,
    chosen,
    qkv_w,
    out_w,
    down_qkv,
    up_qkv,
    down_out,
    up_out,
    stats,
    x,
    part_out,
    part_in,
    part_own,
    low_own,
    low_in,
    mixed_out,
    mixed,
    res_out,
    res_in,
    res_own,
    lowo_out,
    lowo_in,
    lowo_own,
    own_bias,
    load_sem,
    stat_send,
    stat_recv,
    x_send,
    x_recv,
    part_send,
    part_recv,
    low_send,
    low_recv,
    mixed_send,
    mixed_recv,
    chain_send,
    chain_recv,
    res_send,
    res_recv,
    lowo_send,
    lowo_recv,
):
    rows = planes
    r = lax.axis_index("row")
    c = lax.axis_index("col")
    z = c // 2
    k = c % 2
    sib = c + 1 - 2 * k
    block = hidden.shape[0]
    head_col = pl.multiple_of(r * HIDDEN_PART, 128)

    def to(src, dst, send, recv, row, col):
        return pltpu.make_async_remote_copy(
            src_ref=src,
            dst_ref=dst,
            send_sem=send,
            recv_sem=recv,
            device_id=(row, col),
            device_id_type=pl.DeviceIdType.MESH,
        )

    loads = [
        pltpu.make_async_copy(qkv_hbm, qkv_w, load_sem.at[0]),
        pltpu.make_async_copy(down_qkv_hbm, down_qkv, load_sem.at[1]),
        pltpu.make_async_copy(
            up_qkv_hbm.at[:, :, pl.ds(head_col, HIDDEN_PART)], up_qkv, load_sem.at[2]
        ),
        pltpu.make_async_copy(down_out_hbm, down_out, load_sem.at[3]),
        pltpu.make_async_copy(out_hbm, out_w, load_sem.at[4]),
        pltpu.make_async_copy(up_out_hbm, up_out, load_sem.at[5]),
        pltpu.make_async_copy(hidden_hbm, hidden, load_sem.at[6]),
        pltpu.make_async_copy(gain_hbm, gain, load_sem.at[7]),
        pltpu.make_async_copy(shift_hbm, shift, load_sem.at[8]),
        pltpu.make_async_copy(qkv_bias_hbm, qkv_bias, load_sem.at[9]),
        pltpu.make_async_copy(out_bias_hbm, out_bias, load_sem.at[10]),
        pltpu.make_async_copy(prompt_lens_hbm, prompt_lens, load_sem.at[11]),
        pltpu.make_async_copy(suffix_lens_hbm, suffix_lens, load_sem.at[12]),
        pltpu.make_async_copy(group_sizes_hbm, group_sizes, load_sem.at[13]),
        pltpu.make_async_copy(choice_hbm, choice, load_sem.at[14]),
        pltpu.make_async_copy(chosen_hbm, chosen, load_sem.at[15]),
    ]
    for load in loads[6:] + loads[:6]:
        load.start()

    barrier = pltpu.get_barrier_semaphore()

    def greet(row, col):
        pl.semaphore_signal(
            barrier, inc=1, device_id=(row, col), device_id_type=pl.DeviceIdType.MESH
        )

    greet(r, sib)
    for step in range(1, rows):
        greet((r + step) % rows, c)

    @pl.when(z > 0)
    def _():
        greet(r, c - 2)

    @pl.when(z < planes - 1)
    def _():
        greet(r, c + 2)

    before = (z + planes - 1) // planes
    after = (2 * planes - 2 - z) // planes
    pl.semaphore_wait(barrier, rows + before + after)

    loads[6].wait()
    wide = hidden[...].astype(F32)
    width = wide.shape[1]
    own_mean = jnp.mean(wide, axis=1, keepdims=True)
    centred = wide - own_mean
    own_spread = jnp.sum(centred * centred, axis=1, keepdims=True)
    lane = lax.broadcasted_iota(jnp.int32, (block, 128), 1)
    stats[r] = jnp.where(lane == 0, own_mean, own_spread)

    def stat_copy(row):
        return to(stats.at[r], stats.at[r], stat_send.at[row], stat_recv.at[r], row, c)

    for step in range(1, rows):
        stat_copy((r + step) % rows).start()
    for step in range(1, rows):
        peer = (r + step) % rows
        to(stats.at[peer], stats.at[peer], stat_send.at[peer], stat_recv.at[peer], r, c).wait_recv()
    means = [stats[i][:, 0:1] for i in range(rows)]
    average = sum(means) / rows
    spread = sum(stats[i][:, 1:2] for i in range(rows))
    spread = spread + width * sum((m - average) * (m - average) for m in means)
    spread = spread / (width * rows)

    loads[7].wait()
    loads[8].wait()

    def x_rows(index):
        return pl.ds(pl.multiple_of(index * block, 16), block)

    x[x_rows(c), :] = (
        (hidden[...].astype(F32) - average)
        * lax.rsqrt(spread + 1e-05)
        * gain[...].astype(F32)[None]
        + shift[...].astype(F32)[None]
    ).astype(BF)

    def x_copy(way, group, col):
        at = x_rows(2 * group + k)
        return to(
            x.at[at], x.at[at], x_send.at[way, group], x_recv.at[2 * group + k], r, col
        )

    def x_wait(index):
        at = x_rows(index)
        to(x.at[at], x.at[at], x_send.at[0, 0], x_recv.at[index], r, c).wait_recv()

    def part_copy(group, row):
        return to(
            part_out.at[group, row],
            part_in.at[group, r],
            part_send.at[group, row],
            part_recv.at[group, r],
            row,
            c,
        )

    def low_copy(group, row):
        return to(
            low_own.at[group],
            low_in.at[group, r],
            low_send.at[group, row],
            low_recv.at[group, r],
            row,
            c,
        )

    def adapter(group):
        return chosen[choice[group]]

    def token_rows(group):
        return pl.ds(pl.multiple_of(group * GCAP, 16), GCAP)

    def project(group):
        low_own[group] = lax.dot_general(
            down_qkv[adapter(group)],
            x[token_rows(group), :],
            (((1,), (1,)), ((), ())),
            preferred_element_type=F32,
        )
        for step in range(1, rows):
            low_copy(group, (r + step) % rows).start()

        def one(step, _):
            row = (r + step) % rows
            cols = pl.ds(pl.multiple_of(row * HIDDEN_PART, 128), HIDDEN_PART)
            part = jnp.dot(
                x[token_rows(group), :], qkv_w[:, cols], preferred_element_type=F32
            )

            @pl.when(row != r)
            def _():
                part_out[group, row] = part.astype(BF)
                part_copy(group, row).start()

            @pl.when(row == r)
            def _():
                part_own[group] = part

            return 0

        lax.fori_loop(1, rows + 1, one, 0)

    def layout(group, axis):
        shape = (GCAP, 1) if axis == 0 else (1, GCAP)
        offsets = lax.broadcasted_iota(jnp.int32, shape, axis)
        prompt = prompt_lens[group]
        count = group_sizes[group]
        end = prompt
        request = jnp.zeros(shape, jnp.int32)
        begin = jnp.zeros(shape, jnp.int32)
        for j in range(suffix_lens.shape[1]):
            start = end
            end = end + jnp.where(j < count, suffix_lens[group, j], 0)
            passed = jnp.where(offsets >= end, 1, 0)
            begin = begin + jnp.where(offsets >= start, (1 - passed) * start, 0)
            request = request + passed
        inside = offsets < prompt
        position = jnp.where(inside, offsets, prompt + offsets - begin)
        request = jnp.where(inside, -1, jnp.where(request < count, request, -2))
        return offsets, request, position

    def allowed_of(group):
        _, request_q, position_q = layout(group, 0)
        key, request_k, position_k = layout(group, 1)
        square = (GCAP, GCAP)
        rq = jnp.broadcast_to(request_q, square)
        rk = jnp.broadcast_to(request_k, square)
        pq = jnp.broadcast_to(position_q, square)
        pk = jnp.broadcast_to(position_k, square)
        keys = jnp.broadcast_to(key, square)
        shared = (rk == -1) | ((rk == rq) & (rk != -2))
        near = (pq - pk < WIN) | (pk == 0)
        live = shared & (pk <= pq) & near & (rq != -2)
        return live | ((rq == -2) & (keys == 0))

    def mixed_copy(group, row_from):
        return to(
            mixed_out.at[group],
            mixed.at[group, k, pl.ds(0, GCAP), pl.ds(pl.multiple_of(row_from * 128, 128), 128)],
            mixed_send.at[group],
            mixed_recv.at[group, row_from],
            z,
            c,
        )

    def attend(group):
        low = low_own[group]
        proj = part_own[group] + own_bias[...]
        for step in range(1, rows):
            peer = (r + step) % rows
            to(
                low_own.at[group], low_in.at[group, peer],
                low_send.at[group, peer], low_recv.at[group, peer], r, c,
            ).wait_recv()
            low = low + low_in[group, peer]
        for step in range(1, rows):
            peer = (r + step) % rows
            to(
                part_out.at[group, peer], part_in.at[group, peer],
                part_send.at[group, peer], part_recv.at[group, peer], r, c,
            ).wait_recv()
            proj = proj + part_in[group, peer].astype(F32)
        proj = proj + lax.dot_general(
            low.astype(BF), up_qkv[adapter(group)], (((0,), (0,)), ((), ())),
            preferred_element_type=F32,
        )
        query = (proj[:, :HEAD_SIZE] * HEAD_SIZE ** (-0.5)).astype(BF)
        key = proj[:, HEAD_SIZE : 2 * HEAD_SIZE].astype(BF)
        value = proj[:, 2 * HEAD_SIZE :].astype(BF)
        allowed = allowed_of(group)
        scores = lax.dot_general(
            query, key, (((1,), (1,)), ((), ())), preferred_element_type=F32
        )
        scores = jnp.where(allowed, scores, -1e30)
        highest = jnp.max(scores, axis=1, keepdims=True)
        weights = jnp.where(allowed, jnp.exp(scores - highest), 0.0)
        probs = (weights / jnp.sum(weights, axis=1, keepdims=True)).astype(BF)
        rows_mixed = jnp.dot(probs, value, preferred_element_type=F32).astype(BF)

        @pl.when(r == z)
        def _():
            mixed[group, k, pl.ds(0, GCAP), pl.ds(pl.multiple_of(r * 128, 128), 128)] = rows_mixed
            mixed[group, k, pl.ds(GCAP, 16), :] = down_out[adapter(group)]

        @pl.when(r != z)
        def _():
            mixed_out[group] = rows_mixed
            mixed_copy(group, r).start()

    for load in loads[:6] + loads[9:]:
        load.wait()

    def chain_copy(way, group, col):
        return to(
            mixed.at[group, k], mixed.at[group, k],
            chain_send.at[way, group], chain_recv.at[group, k], r, col,
        )

    def chain_wait(group, half):
        to(
            mixed.at[group, half], mixed.at[group, half],
            chain_send.at[0, group], chain_recv.at[group, half], r, c,
        ).wait_recv()

    def res_copy(group):
        return to(res_out.at[group], res_in.at[r], res_send.at[group], res_recv.at[r], group, c)

    def lowo_copy(group):
        return to(
            lowo_out.at[group], lowo_in.at[r], lowo_send.at[group], lowo_recv.at[r], group, c
        )

    half_rows = out_w.shape[0] // 2

    def combine(group):
        @pl.when(z == r)
        def _():
            for step in range(1, rows):
                mixed_copy(group, (r + step) % rows).wait_recv()

        @pl.when(z != r)
        def _():
            chain_wait(group, k)

        @pl.when((z >= r) & (z < planes - 1))
        def _():
            chain_copy(0, group, c + 2).start()

        @pl.when((z <= r) & (z > 0))
        def _():
            chain_copy(1, group, c - 2).start()

        chain_copy(2, group, sib).start()
        chain_wait(group, 1 - k)
        low = jnp.zeros((16, GCAP), F32)
        part = jnp.zeros((GCAP, out_w.shape[1]), F32)
        for half in range(2):
            tokens = mixed[group, half, pl.ds(0, GCAP), :]
            low = low + lax.dot_general(
                mixed[group, half, pl.ds(GCAP, 16), :], tokens, (((1,), (1,)), ((), ())),
                preferred_element_type=F32,
            )
            part = part + jnp.dot(
                tokens, out_w[half * half_rows : (half + 1) * half_rows, :],
                preferred_element_type=F32,
            )

        @pl.when(group != r)
        def _():
            lowo_out[group] = low
            lowo_copy(group).start()
            res_out[group] = part.astype(BF)
            res_copy(group).start()

        @pl.when(group == r)
        def _():
            lowo_own[...] = low
            res_own[...] = part

    bias = qkv_bias[...].astype(F32)[None]
    own_bias[...] = sum(
        jnp.where(r == head, bias[:, head * HIDDEN_PART : (head + 1) * HIDDEN_PART], 0.0)
        for head in range(rows)
    )

    def first(step, _):
        @pl.when(step < planes)
        def _():
            for side in range(2):
                group = z + step * (2 * side - 1)
                valid = (group >= 0) & (group < planes)
                if side == 1:
                    valid = valid & (step > 0)

                @pl.when(valid)
                def _():
                    @pl.when(step > 0)
                    def _():
                        x_wait(2 * group + k)

                    @pl.when((group <= z) & (z < planes - 1))
                    def _():
                        x_copy(0, group, c + 2).start()

                    @pl.when((group >= z) & (z > 0))
                    def _():
                        x_copy(1, group, c - 2).start()

                    x_copy(2, group, sib).start()

            def compute(side, _):
                group = z + step * (2 * side - 1)

                @pl.when((group >= 0) & (group < planes) & (step + 1 - side > 0))
                def _():
                    x_wait(2 * group + 1 - k)
                    project(group)

                return 0

            lax.fori_loop(0, 2, compute, 0)

        @pl.when((step > 0) & (step <= planes))
        def _():
            def mix(side, _):
                group = z + (step - 1) * (2 * side - 1)

                @pl.when((group >= 0) & (group < planes) & (step - side > 0))
                def _():
                    attend(group)

                return 0

            lax.fori_loop(0, 2, mix, 0)

        behind = step - 2 - ((r - z) * (r - z) + planes * planes - 1) // (planes * planes)

        @pl.when((behind >= 0) & (behind < planes))
        def _():
            def join(side, _):
                group = r + behind * (2 * side - 1)

                @pl.when((group >= 0) & (group < planes) & (behind + 1 - side > 0))
                def _():
                    combine(group)

                return 0

            lax.fori_loop(0, 2, join, 0)

        return 0

    lax.fori_loop(0, planes + 3, first, 0)

    _, request, _ = layout(r, 0)
    alive = jnp.where(request != -2, 1.0, 0.0)
    low = lowo_own[...]
    total = res_own[...] + out_bias[...].astype(F32)[None]
    for step in range(1, rows):
        peer = (r + step) % rows
        to(
            lowo_out.at[peer], lowo_in.at[peer], lowo_send.at[peer], lowo_recv.at[peer], r, c
        ).wait_recv()
        low = low + lowo_in[peer]
    for step in range(1, rows):
        peer = (r + step) % rows
        to(
            res_out.at[peer], res_in.at[peer], res_send.at[peer], res_recv.at[peer], r, c
        ).wait_recv()
        total = total + res_in[peer].astype(F32)
    total = total + lax.dot_general(
        low.astype(BF), up_out[adapter(r)], (((0,), (0,)), ((), ())), preferred_element_type=F32
    )
    out[...] = (total * alive).astype(BF)

    for step in range(1, rows):
        peer = (r + step) % rows
        stat_copy(peer).wait_send()
        res_copy(peer).wait_send()
        lowo_copy(peer).wait_send()

    def drain(group, _):
        @pl.when((group <= z) & (z < planes - 1))
        def _():
            x_copy(0, group, c + 2).wait_send()

        @pl.when((group >= z) & (z > 0))
        def _():
            x_copy(1, group, c - 2).wait_send()

        x_copy(2, group, sib).wait_send()
        for step in range(1, rows):
            peer = (r + step) % rows
            low_copy(group, peer).wait_send()
            part_copy(group, peer).wait_send()

        @pl.when(r != z)
        def _():
            mixed_copy(group, r).wait_send()

        @pl.when((z >= r) & (z < planes - 1))
        def _():
            chain_copy(0, group, c + 2).wait_send()

        @pl.when((z <= r) & (z > 0))
        def _():
            chain_copy(1, group, c - 2).wait_send()

        chain_copy(2, group, sib).wait_send()
        return 0

    lax.fori_loop(0, planes, drain, 0)


def fused(
    hidden,
    ln_gain,
    ln_shift,
    qkv_weight,
    qkv_bias,
    out_weight,
    out_bias,
    down_qkv,
    up_qkv,
    down_out,
    up_out,
    prompt_lens,
    suffix_lens,
    group_sizes,
    group_adapter_choice,
    chosen,
):
    groups = lax.axis_size("row")
    block, width = hidden.shape
    out_cols = out_weight.shape[1]
    bank, rank = down_out.shape[0], down_out.shape[1]
    down_t = jnp.transpose(down_qkv, (0, 2, 1))
    vmem = pl.BlockSpec(memory_space=pltpu.VMEM)
    hbm = pl.BlockSpec(memory_space=pl.ANY)
    dma = pltpu.SemaphoreType.DMA
    half = HEAD_SIZE * groups
    macs = groups * GCAP * (qkv_weight.size + out_weight.size)
    return pl.pallas_call(
        functools.partial(fused_kernel, groups),
        out_shape=jax.ShapeDtypeStruct((GCAP, out_cols), BF),
        in_specs=[hbm] * 16,
        out_specs=vmem,
        scratch_shapes=[
            pltpu.VMEM(hidden.shape, BF),
            pltpu.VMEM(ln_gain.shape, BF),
            pltpu.VMEM(ln_shift.shape, BF),
            pltpu.VMEM(qkv_bias.shape, BF),
            pltpu.VMEM(out_bias.shape, BF),
            pltpu.SMEM(prompt_lens.shape, jnp.int32),
            pltpu.SMEM(suffix_lens.shape, jnp.int32),
            pltpu.SMEM(group_sizes.shape, jnp.int32),
            pltpu.SMEM(group_adapter_choice.shape, jnp.int32),
            pltpu.SMEM(chosen.shape, jnp.int32),
            pltpu.VMEM(qkv_weight.shape, BF),
            pltpu.VMEM(out_weight.shape, BF),
            pltpu.VMEM(down_t.shape, BF),
            pltpu.VMEM((bank, rank, HIDDEN_PART), BF),
            pltpu.VMEM(down_out.shape, BF),
            pltpu.VMEM(up_out.shape, BF),
            pltpu.VMEM((groups, block, 128), F32),
            pltpu.VMEM((groups * GCAP, width), BF),
            pltpu.VMEM((groups, groups, GCAP, HIDDEN_PART), BF),
            pltpu.VMEM((groups, groups, GCAP, HIDDEN_PART), BF),
            pltpu.VMEM((groups, GCAP, HIDDEN_PART), F32),
            pltpu.VMEM((groups, rank, GCAP), F32),
            pltpu.VMEM((groups, groups, rank, GCAP), F32),
            pltpu.VMEM((groups, GCAP, HEAD_SIZE), BF),
            pltpu.VMEM((groups, 2, GCAP + rank, half), BF),
            pltpu.VMEM((groups, GCAP, out_cols), BF),
            pltpu.VMEM((groups, GCAP, out_cols), BF),
            pltpu.VMEM((GCAP, out_cols), F32),
            pltpu.VMEM((groups, rank, GCAP), F32),
            pltpu.VMEM((groups, rank, GCAP), F32),
            pltpu.VMEM((rank, GCAP), F32),
            pltpu.VMEM((1, HIDDEN_PART), F32),
            dma((16,)),
            dma((groups,)),
            dma((groups,)),
            dma((3, groups)),
            dma((2 * groups,)),
            dma((groups, groups)),
            dma((groups, groups)),
            dma((groups, groups)),
            dma((groups, groups)),
            dma((groups,)),
            dma((groups, groups)),
            dma((3, groups)),
            dma((groups, 2)),
            dma((groups,)),
            dma((groups,)),
            dma((groups,)),
            dma((groups,)),
        ],
        compiler_params=pltpu.CompilerParams(
            collective_id=0, has_side_effects=True, vmem_limit_bytes=60 * 2**20
        ),
        cost_estimate=pl.CostEstimate(
            flops=2 * macs, bytes_accessed=2 * (qkv_weight.size + out_weight.size), transcendentals=0
        ),
    )(
        hidden,
        ln_gain,
        ln_shift,
        qkv_bias,
        out_bias,
        prompt_lens,
        suffix_lens,
        group_sizes,
        group_adapter_choice,
        chosen,
        qkv_weight,
        out_weight,
        down_t,
        up_qkv,
        down_out,
        up_out,
    )


def block_of(*arrays):
    groups = lax.axis_size("row")
    heads_here = arrays[4].shape[0] // HIDDEN_PART
    if heads_here == groups and lax.axis_size("col") == 2 * groups and arrays[5].shape[1] % 128 == 0:
        return fused(*arrays)
    return local(*arrays)


def solution(mesh):
    in_specs = (
        P("col", "row"),
        P("row"),
        P("row"),
        P("row", "col"),
        P("col"),
        P("row", "col"),
        P("col"),
        P(None, "row", None),
        P(None, None, "col"),
        P(None, None, "col"),
        P(None, None, "col"),
        P(),
        P(),
        P(),
        P(),
        P(),
    )
    out_specs = P("row", "col")
    return jax.shard_map(block_of, mesh=mesh, in_specs=in_specs, out_specs=out_specs, check_vma=False)
```

```python
import functools

import jax
import jax.numpy as jnp
from jax import lax
from jax.experimental import pallas as pl
from jax.experimental.pallas import tpu as pltpu
from jax.sharding import PartitionSpec as P

HEAD_SIZE = 128
GCAP = 160
WIN = 53


def group_layout(prompt, count, suffix):
    offsets = jnp.arange(GCAP, dtype=jnp.int32)
    chosen_adapter_index = jnp.arange(suffix.shape[0], dtype=jnp.int32)
    live_lens = jnp.where(chosen_adapter_index < count, suffix, 0)
    end_at = prompt + jnp.cumsum(live_lens)
    group_start_rows = end_at - live_lens
    request = jnp.sum((offsets[:, None] >= end_at[None, :]).astype(jnp.int32), axis=1)
    in_prompt = offsets < prompt
    live_rows = in_prompt | (request < count)
    group_begin_row = jnp.sum(
        jnp.where(chosen_adapter_index[None, :] == request[:, None], group_start_rows[None, :], 0),
        axis=1,
    )
    position = jnp.where(in_prompt, offsets, prompt + offsets - group_begin_row)
    request_of = jnp.where(in_prompt, -1, request)
    return (live_rows, request_of, position)


def key_mask(live_rows, request_of, position):
    shared = (request_of[None, :] == -1) | (request_of[None, :] == request_of[:, None])
    causal = position[None, :] <= position[:, None]
    within = (position[:, None] - position[None, :] < WIN) | (position[None, :] == 0)
    allowed = live_rows[:, None] & live_rows[None, :] & shared & causal & within
    first_key = jnp.arange(GCAP)[None, :] == 0
    return jnp.where(live_rows[:, None], allowed, first_key)


def attention(queries, key_rows, value_rows, allowed):
    scores = jnp.einsum("qhe,khe->hqk", queries, key_rows, preferred_element_type=jnp.float32)
    scores = jnp.where(allowed[None], scores, -1e30)
    highest = jnp.max(scores, axis=2, keepdims=True)
    weights = jnp.where(allowed[None], jnp.exp(scores - highest), 0.0)
    probs = (weights / jnp.sum(weights, axis=2, keepdims=True)).astype(jnp.bfloat16)
    mixed_rows = jnp.einsum("hqk,khe->qhe", probs, value_rows, preferred_element_type=jnp.float32)
    return mixed_rows.astype(jnp.bfloat16).reshape(queries.shape[0], -1)


def normalise(hidden, ln_gain, ln_shift):
    widened = hidden.astype(jnp.float32)
    width = widened.shape[1]
    own_mean = jnp.mean(widened, axis=1, keepdims=True)
    centred = widened - own_mean
    own_spread = jnp.sum(centred * centred, axis=1, keepdims=True)
    every = lax.all_gather(jnp.concatenate([own_mean, own_spread], axis=1), "row", axis=0)
    means, spreads = every[:, :, :1], every[:, :, 1:]
    average = jnp.mean(means, axis=0)
    between = jnp.sum((means - average) * (means - average), axis=0) * width
    spread = (jnp.sum(spreads, axis=0) + between) / (width * every.shape[0])
    return (
        (widened - average) * lax.rsqrt(spread + 1e-05) * ln_gain.astype(jnp.float32)
        + ln_shift.astype(jnp.float32)
    ).astype(jnp.bfloat16)


def sum_over_row(partial):
    moved = lax.all_to_all(partial, "row", split_axis=0, concat_axis=0, tiled=True)
    blocks = moved.reshape((lax.axis_size("row"), -1) + moved.shape[1:])
    return jnp.sum(blocks.astype(jnp.float32), axis=0)


def local(
    hidden,
    ln_gain,
    ln_shift,
    qkv_weight,
    qkv_bias,
    out_weight,
    out_bias,
    down_qkv,
    up_qkv,
    down_out,
    up_out,
    prompt_lens,
    suffix_lens,
    group_sizes,
    group_adapter_choice,
    chosen,
):
    row_index = lax.axis_index("row")
    groups = lax.axis_size("row")
    adapters = chosen[group_adapter_choice]
    own_adapter = adapters[row_index]
    normed = normalise(hidden, ln_gain, ln_shift)
    tokens = lax.all_gather(normed, "col", axis=0, tiled=True)
    low_part = jnp.einsum(
        "gtd,gdr->gtr",
        tokens.reshape(groups, GCAP, -1),
        down_qkv[adapters],
        preferred_element_type=jnp.float32,
    )
    low = sum_over_row(low_part.reshape(groups * GCAP, -1)).astype(jnp.bfloat16)
    part = jnp.dot(tokens, qkv_weight, preferred_element_type=jnp.float32).astype(jnp.bfloat16)
    projected = (
        sum_over_row(part)
        + qkv_bias.astype(jnp.float32)
        + jnp.dot(low, up_qkv[own_adapter], preferred_element_type=jnp.float32)
    )
    heads_here = projected.shape[1] // (3 * HEAD_SIZE)
    shaped = projected.reshape(GCAP, heads_here, 3, HEAD_SIZE)
    queries = (shaped[:, :, 0] * HEAD_SIZE ** (-0.5)).astype(jnp.bfloat16)
    key_rows = shaped[:, :, 1].astype(jnp.bfloat16)
    value_rows = shaped[:, :, 2].astype(jnp.bfloat16)
    live_rows, request_of, position = group_layout(
        prompt_lens[row_index], group_sizes[row_index], suffix_lens[row_index]
    )
    mixed_rows = attention(queries, key_rows, value_rows, key_mask(live_rows, request_of, position))
    all_heads = lax.all_gather(mixed_rows, "col", axis=1, tiled=True)
    down_full = lax.all_gather(down_out[own_adapter], "col", axis=1, tiled=True)
    reduced_out = lax.dot_general(
        all_heads, down_full, (((1,), (1,)), ((), ())), preferred_element_type=jnp.float32
    ).astype(jnp.bfloat16)
    gathered = lax.all_to_all(all_heads, "row", split_axis=1, concat_axis=0, tiled=True)
    out_part = jnp.dot(gathered, out_weight, preferred_element_type=jnp.float32)
    result = (
        sum_over_row(out_part.astype(jnp.bfloat16))
        + out_bias.astype(jnp.float32)
        + jnp.dot(reduced_out, up_out[own_adapter], preferred_element_type=jnp.float32)
    )
    return (result * live_rows[:, None].astype(jnp.float32)).astype(jnp.bfloat16)


HIDDEN_PART = 3 * HEAD_SIZE
BF = jnp.bfloat16
F32 = jnp.float32


def fused_kernel(
    planes,
    hidden_hbm,
    gain_hbm,
    shift_hbm,
    qkv_bias_hbm,
    out_bias_hbm,
    prompt_lens_hbm,
    suffix_lens_hbm,
    group_sizes_hbm,
    choice_hbm,
    chosen_hbm,
    qkv_hbm,
    out_hbm,
    down_qkv_hbm,
    up_qkv_hbm,
    down_out_hbm,
    up_out_hbm,
    out,
    hidden,
    gain,
    shift,
    qkv_bias,
    out_bias,
    prompt_lens,
    suffix_lens,
    group_sizes,
    choice,
    chosen,
    qkv_w,
    out_w,
    down_qkv,
    up_qkv,
    down_out,
    up_out,
    stats,
    x,
    part_out,
    part_in,
    part_own,
    low_own,
    low_in,
    mixed_out,
    mixed,
    res_out,
    res_in,
    res_own,
    lowo_out,
    lowo_in,
    lowo_own,
    own_bias,
    load_sem,
    stat_send,
    stat_recv,
    x_send,
    x_recv,
    part_send,
    part_recv,
    low_send,
    low_recv,
    mixed_send,
    mixed_recv,
    chain_send,
    chain_recv,
    res_send,
    res_recv,
    lowo_send,
    lowo_recv,
):
    rows = planes
    r = lax.axis_index("row")
    c = lax.axis_index("col")
    z = c // 2
    k = c % 2
    sib = c + 1 - 2 * k
    block = hidden.shape[0]
    head_col = pl.multiple_of(r * HIDDEN_PART, 128)

    def to(src, dst, send, recv, row, col):
        return pltpu.make_async_remote_copy(
            src_ref=src,
            dst_ref=dst,
            send_sem=send,
            recv_sem=recv,
            device_id=(row, col),
            device_id_type=pl.DeviceIdType.MESH,
        )

    loads = [
        pltpu.make_async_copy(qkv_hbm, qkv_w, load_sem.at[0]),
        pltpu.make_async_copy(down_qkv_hbm, down_qkv, load_sem.at[1]),
        pltpu.make_async_copy(
            up_qkv_hbm.at[:, :, pl.ds(head_col, HIDDEN_PART)], up_qkv, load_sem.at[2]
        ),
        pltpu.make_async_copy(down_out_hbm, down_out, load_sem.at[3]),
        pltpu.make_async_copy(out_hbm, out_w, load_sem.at[4]),
        pltpu.make_async_copy(up_out_hbm, up_out, load_sem.at[5]),
        pltpu.make_async_copy(hidden_hbm, hidden, load_sem.at[6]),
        pltpu.make_async_copy(gain_hbm, gain, load_sem.at[7]),
        pltpu.make_async_copy(shift_hbm, shift, load_sem.at[8]),
        pltpu.make_async_copy(qkv_bias_hbm, qkv_bias, load_sem.at[9]),
        pltpu.make_async_copy(out_bias_hbm, out_bias, load_sem.at[10]),
        pltpu.make_async_copy(prompt_lens_hbm, prompt_lens, load_sem.at[11]),
        pltpu.make_async_copy(suffix_lens_hbm, suffix_lens, load_sem.at[12]),
        pltpu.make_async_copy(group_sizes_hbm, group_sizes, load_sem.at[13]),
        pltpu.make_async_copy(choice_hbm, choice, load_sem.at[14]),
        pltpu.make_async_copy(chosen_hbm, chosen, load_sem.at[15]),
    ]
    for load in loads[6:] + loads[:6]:
        load.start()

    barrier = pltpu.get_barrier_semaphore()

    def greet(row, col):
        pl.semaphore_signal(
            barrier, inc=1, device_id=(row, col), device_id_type=pl.DeviceIdType.MESH
        )

    greet(r, sib)
    for step in range(1, rows):
        greet((r + step) % rows, c)

    @pl.when(z > 0)
    def _():
        greet(r, c - 2)

    @pl.when(z < planes - 1)
    def _():
        greet(r, c + 2)

    before = (z + planes - 1) // planes
    after = (2 * planes - 2 - z) // planes
    pl.semaphore_wait(barrier, rows + before + after)

    loads[6].wait()
    wide = hidden[...].astype(F32)
    width = wide.shape[1]
    own_mean = jnp.mean(wide, axis=1, keepdims=True)
    centred = wide - own_mean
    own_spread = jnp.sum(centred * centred, axis=1, keepdims=True)
    lane = lax.broadcasted_iota(jnp.int32, (block, 128), 1)
    stats[r] = jnp.where(lane == 0, own_mean, own_spread)

    def stat_copy(row):
        return to(stats.at[r], stats.at[r], stat_send.at[row], stat_recv.at[r], row, c)

    for step in range(1, rows):
        stat_copy((r + step) % rows).start()
    for step in range(1, rows):
        peer = (r + step) % rows
        to(stats.at[peer], stats.at[peer], stat_send.at[peer], stat_recv.at[peer], r, c).wait_recv()
    means = [stats[i][:, 0:1] for i in range(rows)]
    average = sum(means) / rows
    spread = sum(stats[i][:, 1:2] for i in range(rows))
    spread = spread + width * sum((m - average) * (m - average) for m in means)
    spread = spread / (width * rows)

    loads[7].wait()
    loads[8].wait()

    def x_rows(index):
        return pl.ds(pl.multiple_of(index * block, 16), block)

    x[x_rows(c), :] = (
        (hidden[...].astype(F32) - average)
        * lax.rsqrt(spread + 1e-05)
        * gain[...].astype(F32)[None]
        + shift[...].astype(F32)[None]
    ).astype(BF)

    def x_copy(way, group, col):
        at = x_rows(2 * group + k)
        return to(
            x.at[at], x.at[at], x_send.at[way, group], x_recv.at[2 * group + k], r, col
        )

    def x_wait(index):
        at = x_rows(index)
        to(x.at[at], x.at[at], x_send.at[0, 0], x_recv.at[index], r, c).wait_recv()

    def part_copy(group, row):
        return to(
            part_out.at[group, row],
            part_in.at[group, r],
            part_send.at[group, row],
            part_recv.at[group, r],
            row,
            c,
        )

    def low_copy(group, row):
        return to(
            low_own.at[group],
            low_in.at[group, r],
            low_send.at[group, row],
            low_recv.at[group, r],
            row,
            c,
        )

    def adapter(group):
        return chosen[choice[group]]

    def token_rows(group):
        return pl.ds(pl.multiple_of(group * GCAP, 16), GCAP)

    def project(group):
        low_own[group] = lax.dot_general(
            down_qkv[adapter(group)],
            x[token_rows(group), :],
            (((1,), (1,)), ((), ())),
            preferred_element_type=F32,
        )
        for step in range(1, rows):
            low_copy(group, (r + step) % rows).start()

        def one(step, _):
            row = (r + step) % rows
            cols = pl.ds(pl.multiple_of(row * HIDDEN_PART, 128), HIDDEN_PART)
            part = jnp.dot(
                x[token_rows(group), :], qkv_w[:, cols], preferred_element_type=F32
            )

            @pl.when(row != r)
            def _():
                part_out[group, row] = part.astype(BF)
                part_copy(group, row).start()

            @pl.when(row == r)
            def _():
                part_own[group] = part

            return 0

        lax.fori_loop(1, rows + 1, one, 0)

    def layout(group, axis):
        shape = (GCAP, 1) if axis == 0 else (1, GCAP)
        offsets = lax.broadcasted_iota(jnp.int32, shape, axis)
        prompt = prompt_lens[group]
        count = group_sizes[group]
        end = prompt
        request = jnp.zeros(shape, jnp.int32)
        begin = jnp.zeros(shape, jnp.int32)
        for j in range(suffix_lens.shape[1]):
            start = end
            end = end + jnp.where(j < count, suffix_lens[group, j], 0)
            passed = jnp.where(offsets >= end, 1, 0)
            begin = begin + jnp.where(offsets >= start, (1 - passed) * start, 0)
            request = request + passed
        inside = offsets < prompt
        position = jnp.where(inside, offsets, prompt + offsets - begin)
        request = jnp.where(inside, -1, jnp.where(request < count, request, -2))
        return offsets, request, position

    def allowed_of(group):
        _, request_q, position_q = layout(group, 0)
        key, request_k, position_k = layout(group, 1)
        square = (GCAP, GCAP)
        rq = jnp.broadcast_to(request_q, square)
        rk = jnp.broadcast_to(request_k, square)
        pq = jnp.broadcast_to(position_q, square)
        pk = jnp.broadcast_to(position_k, square)
        keys = jnp.broadcast_to(key, square)
        shared = (rk == -1) | ((rk == rq) & (rk != -2))
        near = (pq - pk < WIN) | (pk == 0)
        live = shared & (pk <= pq) & near & (rq != -2)
        return live | ((rq == -2) & (keys == 0))

    def mixed_copy(group, row_from):
        return to(
            mixed_out.at[group],
            mixed.at[group, k, pl.ds(0, GCAP), pl.ds(pl.multiple_of(row_from * 128, 128), 128)],
            mixed_send.at[group],
            mixed_recv.at[group, row_from],
            z,
            c,
        )

    def attend(group):
        low = low_own[group]
        proj = part_own[group] + own_bias[...]
        for step in range(1, rows):
            peer = (r + step) % rows
            to(
                low_own.at[group], low_in.at[group, peer],
                low_send.at[group, peer], low_recv.at[group, peer], r, c,
            ).wait_recv()
            low = low + low_in[group, peer]
        for step in range(1, rows):
            peer = (r + step) % rows
            to(
                part_out.at[group, peer], part_in.at[group, peer],
                part_send.at[group, peer], part_recv.at[group, peer], r, c,
            ).wait_recv()
            proj = proj + part_in[group, peer].astype(F32)
        proj = proj + lax.dot_general(
            low.astype(BF), up_qkv[adapter(group)], (((0,), (0,)), ((), ())),
            preferred_element_type=F32,
        )
        query = (proj[:, :HEAD_SIZE] * HEAD_SIZE ** (-0.5)).astype(BF)
        key = proj[:, HEAD_SIZE : 2 * HEAD_SIZE].astype(BF)
        value = proj[:, 2 * HEAD_SIZE :].astype(BF)
        allowed = allowed_of(group)
        scores = lax.dot_general(
            query, key, (((1,), (1,)), ((), ())), preferred_element_type=F32
        )
        scores = jnp.where(allowed, scores, -1e30)
        highest = jnp.max(scores, axis=1, keepdims=True)
        weights = jnp.where(allowed, jnp.exp(scores - highest), 0.0)
        probs = (weights / jnp.sum(weights, axis=1, keepdims=True)).astype(BF)
        rows_mixed = jnp.dot(probs, value, preferred_element_type=F32).astype(BF)

        @pl.when(r == z)
        def _():
            mixed[group, k, pl.ds(0, GCAP), pl.ds(pl.multiple_of(r * 128, 128), 128)] = rows_mixed
            mixed[group, k, pl.ds(GCAP, 16), :] = down_out[adapter(group)]

        @pl.when(r != z)
        def _():
            mixed_out[group] = rows_mixed
            mixed_copy(group, r).start()

    for load in loads[9:]:
        load.wait()

    parts = chain_recv.shape[2]
    part_width = mixed.shape[3] // parts

    def chain_at(group, half, part):
        return mixed.at[group, half, :, pl.ds(part * part_width, part_width)]

    def chain_copy(way, group, part, col):
        return to(
            chain_at(group, k, part), chain_at(group, k, part),
            chain_send.at[way, group, part], chain_recv.at[group, k, part], r, col,
        )

    def chain_wait(group, half, part):
        to(
            chain_at(group, half, part), chain_at(group, half, part),
            chain_send.at[0, group, part], chain_recv.at[group, half, part], r, c,
        ).wait_recv()

    def res_copy(group):
        return to(res_out.at[group], res_in.at[r], res_send.at[group], res_recv.at[r], group, c)

    def lowo_copy(group):
        return to(
            lowo_out.at[group], lowo_in.at[r], lowo_send.at[group], lowo_recv.at[r], group, c
        )

    half_rows = out_w.shape[0] // 2

    def combine(group):
        @pl.when(z == r)
        def _():
            for step in range(1, rows):
                mixed_copy(group, (r + step) % rows).wait_recv()

        for part in range(parts):
            @pl.when(z != r)
            def _():
                chain_wait(group, k, part)

            @pl.when((z >= r) & (z < planes - 1))
            def _():
                chain_copy(0, group, part, c + 2).start()

            @pl.when((z <= r) & (z > 0))
            def _():
                chain_copy(1, group, part, c - 2).start()

            chain_copy(2, group, part, sib).start()
        for part in range(parts):
            chain_wait(group, 1 - k, part)
        low = jnp.zeros((16, GCAP), F32)
        part = jnp.zeros((GCAP, out_w.shape[1]), F32)
        for half in range(2):
            tokens = mixed[group, half, pl.ds(0, GCAP), :]
            low = low + lax.dot_general(
                mixed[group, half, pl.ds(GCAP, 16), :], tokens, (((1,), (1,)), ((), ())),
                preferred_element_type=F32,
            )
            part = part + jnp.dot(
                tokens, out_w[half * half_rows : (half + 1) * half_rows, :],
                preferred_element_type=F32,
            )

        @pl.when(group != r)
        def _():
            lowo_out[group] = low
            lowo_copy(group).start()
            res_out[group] = part.astype(BF)
            res_copy(group).start()

        @pl.when(group == r)
        def _():
            lowo_own[...] = low
            res_own[...] = part

    bias = qkv_bias[...].astype(F32)[None]
    own_bias[...] = sum(
        jnp.where(r == head, bias[:, head * HIDDEN_PART : (head + 1) * HIDDEN_PART], 0.0)
        for head in range(rows)
    )

    def first(step, _):
        @pl.when(step < planes)
        def _():
            for side in range(2):
                group = z + step * (2 * side - 1)
                valid = (group >= 0) & (group < planes)
                if side == 1:
                    valid = valid & (step > 0)

                @pl.when(valid)
                def _():
                    @pl.when(step > 0)
                    def _():
                        x_wait(2 * group + k)

                    @pl.when((group <= z) & (z < planes - 1))
                    def _():
                        x_copy(0, group, c + 2).start()

                    @pl.when((group >= z) & (z > 0))
                    def _():
                        x_copy(1, group, c - 2).start()

                    x_copy(2, group, sib).start()

            @pl.when(step == 0)
            def _():
                for load in loads[:6]:
                    load.wait()

            def compute(side, _):
                group = z + step * (2 * side - 1)

                @pl.when((group >= 0) & (group < planes) & (step + 1 - side > 0))
                def _():
                    x_wait(2 * group + 1 - k)
                    project(group)

                return 0

            lax.fori_loop(0, 2, compute, 0)

        behind = step - 2 - ((r - z) * (r - z) + planes * planes - 1) // (planes * planes)

        @pl.when((behind >= 0) & (behind < planes))
        def _():
            def join(side, _):
                group = r + behind * (2 * side - 1)

                @pl.when((group >= 0) & (group < planes) & (behind + 1 - side > 0))
                def _():
                    combine(group)

                return 0

            lax.fori_loop(0, 2, join, 0)

        @pl.when((step > 0) & (step <= planes))
        def _():
            def mix(side, _):
                group = z + (step - 1) * (2 * side - 1)

                @pl.when((group >= 0) & (group < planes) & (step - side > 0))
                def _():
                    attend(group)

                return 0

            lax.fori_loop(0, 2, mix, 0)

        return 0

    lax.fori_loop(0, planes + 3, first, 0)

    _, request, _ = layout(r, 0)
    alive = jnp.where(request != -2, 1.0, 0.0)
    low = lowo_own[...]
    total = res_own[...] + out_bias[...].astype(F32)[None]
    for step in range(1, rows):
        peer = (r + step) % rows
        to(
            lowo_out.at[peer], lowo_in.at[peer], lowo_send.at[peer], lowo_recv.at[peer], r, c
        ).wait_recv()
        low = low + lowo_in[peer]
    for step in range(1, rows):
        peer = (r + step) % rows
        to(
            res_out.at[peer], res_in.at[peer], res_send.at[peer], res_recv.at[peer], r, c
        ).wait_recv()
        total = total + res_in[peer].astype(F32)
    total = total + lax.dot_general(
        low.astype(BF), up_out[adapter(r)], (((0,), (0,)), ((), ())), preferred_element_type=F32
    )
    out[...] = (total * alive).astype(BF)

    for step in range(1, rows):
        peer = (r + step) % rows
        stat_copy(peer).wait_send()
        res_copy(peer).wait_send()
        lowo_copy(peer).wait_send()

    def drain(group, _):
        @pl.when((group <= z) & (z < planes - 1))
        def _():
            x_copy(0, group, c + 2).wait_send()

        @pl.when((group >= z) & (z > 0))
        def _():
            x_copy(1, group, c - 2).wait_send()

        x_copy(2, group, sib).wait_send()
        for step in range(1, rows):
            peer = (r + step) % rows
            low_copy(group, peer).wait_send()
            part_copy(group, peer).wait_send()

        @pl.when(r != z)
        def _():
            mixed_copy(group, r).wait_send()

        for part in range(parts):
            @pl.when((z >= r) & (z < planes - 1))
            def _():
                chain_copy(0, group, part, c + 2).wait_send()

            @pl.when((z <= r) & (z > 0))
            def _():
                chain_copy(1, group, part, c - 2).wait_send()

            chain_copy(2, group, part, sib).wait_send()
        return 0

    lax.fori_loop(0, planes, drain, 0)


def fused(
    hidden,
    ln_gain,
    ln_shift,
    qkv_weight,
    qkv_bias,
    out_weight,
    out_bias,
    down_qkv,
    up_qkv,
    down_out,
    up_out,
    prompt_lens,
    suffix_lens,
    group_sizes,
    group_adapter_choice,
    chosen,
):
    groups = lax.axis_size("row")
    block, width = hidden.shape
    out_cols = out_weight.shape[1]
    bank, rank = down_out.shape[0], down_out.shape[1]
    down_t = jnp.transpose(down_qkv, (0, 2, 1))
    vmem = pl.BlockSpec(memory_space=pltpu.VMEM)
    hbm = pl.BlockSpec(memory_space=pl.ANY)
    dma = pltpu.SemaphoreType.DMA
    half = HEAD_SIZE * groups
    macs = groups * GCAP * (qkv_weight.size + out_weight.size)
    return pl.pallas_call(
        functools.partial(fused_kernel, groups),
        out_shape=jax.ShapeDtypeStruct((GCAP, out_cols), BF),
        in_specs=[hbm] * 16,
        out_specs=vmem,
        scratch_shapes=[
            pltpu.VMEM(hidden.shape, BF),
            pltpu.VMEM(ln_gain.shape, BF),
            pltpu.VMEM(ln_shift.shape, BF),
            pltpu.VMEM(qkv_bias.shape, BF),
            pltpu.VMEM(out_bias.shape, BF),
            pltpu.SMEM(prompt_lens.shape, jnp.int32),
            pltpu.SMEM(suffix_lens.shape, jnp.int32),
            pltpu.SMEM(group_sizes.shape, jnp.int32),
            pltpu.SMEM(group_adapter_choice.shape, jnp.int32),
            pltpu.SMEM(chosen.shape, jnp.int32),
            pltpu.VMEM(qkv_weight.shape, BF),
            pltpu.VMEM(out_weight.shape, BF),
            pltpu.VMEM(down_t.shape, BF),
            pltpu.VMEM((bank, rank, HIDDEN_PART), BF),
            pltpu.VMEM(down_out.shape, BF),
            pltpu.VMEM(up_out.shape, BF),
            pltpu.VMEM((groups, block, 128), F32),
            pltpu.VMEM((groups * GCAP, width), BF),
            pltpu.VMEM((groups, groups, GCAP, HIDDEN_PART), BF),
            pltpu.VMEM((groups, groups, GCAP, HIDDEN_PART), BF),
            pltpu.VMEM((groups, GCAP, HIDDEN_PART), F32),
            pltpu.VMEM((groups, rank, GCAP), F32),
            pltpu.VMEM((groups, groups, rank, GCAP), F32),
            pltpu.VMEM((groups, GCAP, HEAD_SIZE), BF),
            pltpu.VMEM((groups, 2, GCAP + rank, half), BF),
            pltpu.VMEM((groups, GCAP, out_cols), BF),
            pltpu.VMEM((groups, GCAP, out_cols), BF),
            pltpu.VMEM((GCAP, out_cols), F32),
            pltpu.VMEM((groups, rank, GCAP), F32),
            pltpu.VMEM((groups, rank, GCAP), F32),
            pltpu.VMEM((rank, GCAP), F32),
            pltpu.VMEM((1, HIDDEN_PART), F32),
            dma((16,)),
            dma((groups,)),
            dma((groups,)),
            dma((3, groups)),
            dma((2 * groups,)),
            dma((groups, groups)),
            dma((groups, groups)),
            dma((groups, groups)),
            dma((groups, groups)),
            dma((groups,)),
            dma((groups, groups)),
            dma((3, groups, 2)),
            dma((groups, 2, 2)),
            dma((groups,)),
            dma((groups,)),
            dma((groups,)),
            dma((groups,)),
        ],
        compiler_params=pltpu.CompilerParams(
            collective_id=0, has_side_effects=True, vmem_limit_bytes=60 * 2**20
        ),
        cost_estimate=pl.CostEstimate(
            flops=2 * macs, bytes_accessed=2 * (qkv_weight.size + out_weight.size), transcendentals=0
        ),
    )(
        hidden,
        ln_gain,
        ln_shift,
        qkv_bias,
        out_bias,
        prompt_lens,
        suffix_lens,
        group_sizes,
        group_adapter_choice,
        chosen,
        qkv_weight,
        out_weight,
        down_t,
        up_qkv,
        down_out,
        up_out,
    )


def block_of(*arrays):
    groups = lax.axis_size("row")
    heads_here = arrays[4].shape[0] // HIDDEN_PART
    if heads_here == groups and lax.axis_size("col") == 2 * groups and arrays[5].shape[1] % 128 == 0:
        return fused(*arrays)
    return local(*arrays)


def solution(mesh):
    in_specs = (
        P("col", "row"),
        P("row"),
        P("row"),
        P("row", "col"),
        P("col"),
        P("row", "col"),
        P("col"),
        P(None, "row", None),
        P(None, None, "col"),
        P(None, None, "col"),
        P(None, None, "col"),
        P(),
        P(),
        P(),
        P(),
        P(),
    )
    out_specs = P("row", "col")
    return jax.shard_map(block_of, mesh=mesh, in_specs=in_specs, out_specs=out_specs, check_vma=False)
```

```python
import functools

import jax
import jax.numpy as jnp
from jax import lax
from jax.experimental import pallas as pl
from jax.experimental.pallas import tpu as pltpu
from jax.sharding import PartitionSpec as P

HEAD_SIZE = 128
GCAP = 160
WIN = 53


def group_layout(prompt, count, suffix):
    offsets = jnp.arange(GCAP, dtype=jnp.int32)
    chosen_adapter_index = jnp.arange(suffix.shape[0], dtype=jnp.int32)
    live_lens = jnp.where(chosen_adapter_index < count, suffix, 0)
    end_at = prompt + jnp.cumsum(live_lens)
    group_start_rows = end_at - live_lens
    request = jnp.sum((offsets[:, None] >= end_at[None, :]).astype(jnp.int32), axis=1)
    in_prompt = offsets < prompt
    live_rows = in_prompt | (request < count)
    group_begin_row = jnp.sum(
        jnp.where(chosen_adapter_index[None, :] == request[:, None], group_start_rows[None, :], 0),
        axis=1,
    )
    position = jnp.where(in_prompt, offsets, prompt + offsets - group_begin_row)
    request_of = jnp.where(in_prompt, -1, request)
    return (live_rows, request_of, position)


def key_mask(live_rows, request_of, position):
    shared = (request_of[None, :] == -1) | (request_of[None, :] == request_of[:, None])
    causal = position[None, :] <= position[:, None]
    within = (position[:, None] - position[None, :] < WIN) | (position[None, :] == 0)
    allowed = live_rows[:, None] & live_rows[None, :] & shared & causal & within
    first_key = jnp.arange(GCAP)[None, :] == 0
    return jnp.where(live_rows[:, None], allowed, first_key)


def attention(queries, key_rows, value_rows, allowed):
    scores = jnp.einsum("qhe,khe->hqk", queries, key_rows, preferred_element_type=jnp.float32)
    scores = jnp.where(allowed[None], scores, -1e30)
    highest = jnp.max(scores, axis=2, keepdims=True)
    weights = jnp.where(allowed[None], jnp.exp(scores - highest), 0.0)
    probs = (weights / jnp.sum(weights, axis=2, keepdims=True)).astype(jnp.bfloat16)
    mixed_rows = jnp.einsum("hqk,khe->qhe", probs, value_rows, preferred_element_type=jnp.float32)
    return mixed_rows.astype(jnp.bfloat16).reshape(queries.shape[0], -1)


def normalise(hidden, ln_gain, ln_shift):
    widened = hidden.astype(jnp.float32)
    width = widened.shape[1]
    own_mean = jnp.mean(widened, axis=1, keepdims=True)
    centred = widened - own_mean
    own_spread = jnp.sum(centred * centred, axis=1, keepdims=True)
    every = lax.all_gather(jnp.concatenate([own_mean, own_spread], axis=1), "row", axis=0)
    means, spreads = every[:, :, :1], every[:, :, 1:]
    average = jnp.mean(means, axis=0)
    between = jnp.sum((means - average) * (means - average), axis=0) * width
    spread = (jnp.sum(spreads, axis=0) + between) / (width * every.shape[0])
    return (
        (widened - average) * lax.rsqrt(spread + 1e-05) * ln_gain.astype(jnp.float32)
        + ln_shift.astype(jnp.float32)
    ).astype(jnp.bfloat16)


def sum_over_row(partial):
    moved = lax.all_to_all(partial, "row", split_axis=0, concat_axis=0, tiled=True)
    blocks = moved.reshape((lax.axis_size("row"), -1) + moved.shape[1:])
    return jnp.sum(blocks.astype(jnp.float32), axis=0)


def local(
    hidden,
    ln_gain,
    ln_shift,
    qkv_weight,
    qkv_bias,
    out_weight,
    out_bias,
    down_qkv,
    up_qkv,
    down_out,
    up_out,
    prompt_lens,
    suffix_lens,
    group_sizes,
    group_adapter_choice,
    chosen,
):
    row_index = lax.axis_index("row")
    groups = lax.axis_size("row")
    adapters = chosen[group_adapter_choice]
    own_adapter = adapters[row_index]
    normed = normalise(hidden, ln_gain, ln_shift)
    tokens = lax.all_gather(normed, "col", axis=0, tiled=True)
    low_part = jnp.einsum(
        "gtd,gdr->gtr",
        tokens.reshape(groups, GCAP, -1),
        down_qkv[adapters],
        preferred_element_type=jnp.float32,
    )
    low = sum_over_row(low_part.reshape(groups * GCAP, -1)).astype(jnp.bfloat16)
    part = jnp.dot(tokens, qkv_weight, preferred_element_type=jnp.float32).astype(jnp.bfloat16)
    projected = (
        sum_over_row(part)
        + qkv_bias.astype(jnp.float32)
        + jnp.dot(low, up_qkv[own_adapter], preferred_element_type=jnp.float32)
    )
    heads_here = projected.shape[1] // (3 * HEAD_SIZE)
    shaped = projected.reshape(GCAP, heads_here, 3, HEAD_SIZE)
    queries = (shaped[:, :, 0] * HEAD_SIZE ** (-0.5)).astype(jnp.bfloat16)
    key_rows = shaped[:, :, 1].astype(jnp.bfloat16)
    value_rows = shaped[:, :, 2].astype(jnp.bfloat16)
    live_rows, request_of, position = group_layout(
        prompt_lens[row_index], group_sizes[row_index], suffix_lens[row_index]
    )
    mixed_rows = attention(queries, key_rows, value_rows, key_mask(live_rows, request_of, position))
    all_heads = lax.all_gather(mixed_rows, "col", axis=1, tiled=True)
    down_full = lax.all_gather(down_out[own_adapter], "col", axis=1, tiled=True)
    reduced_out = lax.dot_general(
        all_heads, down_full, (((1,), (1,)), ((), ())), preferred_element_type=jnp.float32
    ).astype(jnp.bfloat16)
    gathered = lax.all_to_all(all_heads, "row", split_axis=1, concat_axis=0, tiled=True)
    out_part = jnp.dot(gathered, out_weight, preferred_element_type=jnp.float32)
    result = (
        sum_over_row(out_part.astype(jnp.bfloat16))
        + out_bias.astype(jnp.float32)
        + jnp.dot(reduced_out, up_out[own_adapter], preferred_element_type=jnp.float32)
    )
    return (result * live_rows[:, None].astype(jnp.float32)).astype(jnp.bfloat16)


HIDDEN_PART = 3 * HEAD_SIZE
BF = jnp.bfloat16
F32 = jnp.float32


def fused_kernel(
    planes,
    hidden_hbm,
    gain_hbm,
    shift_hbm,
    qkv_bias_hbm,
    out_bias_hbm,
    prompt_lens_hbm,
    suffix_lens_hbm,
    group_sizes_hbm,
    choice_hbm,
    chosen_hbm,
    qkv_hbm,
    out_hbm,
    down_qkv_hbm,
    up_qkv_hbm,
    down_out_hbm,
    up_out_hbm,
    out,
    hidden,
    gain,
    shift,
    qkv_bias,
    out_bias,
    prompt_lens,
    suffix_lens,
    group_sizes,
    choice,
    chosen,
    qkv_w,
    out_w,
    down_qkv,
    up_qkv,
    down_out,
    up_out,
    stats,
    x,
    part_out,
    part_in,
    part_own,
    low_own,
    low_in,
    mixed_out,
    mixed,
    res_out,
    res_in,
    res_own,
    lowo_out,
    lowo_in,
    lowo_own,
    own_bias,
    load_sem,
    stat_send,
    stat_recv,
    x_send,
    x_recv,
    part_send,
    part_recv,
    low_send,
    low_recv,
    mixed_send,
    mixed_recv,
    chain_send,
    chain_recv,
    res_send,
    res_recv,
    lowo_send,
    lowo_recv,
):
    rows = planes
    r = lax.axis_index("row")
    c = lax.axis_index("col")
    z = c // 2
    k = c % 2
    sib = c + 1 - 2 * k
    block = hidden.shape[0]
    head_col = pl.multiple_of(r * HIDDEN_PART, 128)

    def to(src, dst, send, recv, row, col):
        return pltpu.make_async_remote_copy(
            src_ref=src,
            dst_ref=dst,
            send_sem=send,
            recv_sem=recv,
            device_id=(row, col),
            device_id_type=pl.DeviceIdType.MESH,
        )

    loads = [
        pltpu.make_async_copy(qkv_hbm, qkv_w, load_sem.at[0]),
        pltpu.make_async_copy(down_qkv_hbm, down_qkv, load_sem.at[1]),
        pltpu.make_async_copy(
            up_qkv_hbm.at[:, :, pl.ds(head_col, HIDDEN_PART)], up_qkv, load_sem.at[2]
        ),
        pltpu.make_async_copy(down_out_hbm, down_out, load_sem.at[3]),
        pltpu.make_async_copy(out_hbm, out_w, load_sem.at[4]),
        pltpu.make_async_copy(up_out_hbm, up_out, load_sem.at[5]),
        pltpu.make_async_copy(hidden_hbm, hidden, load_sem.at[6]),
        pltpu.make_async_copy(gain_hbm, gain, load_sem.at[7]),
        pltpu.make_async_copy(shift_hbm, shift, load_sem.at[8]),
        pltpu.make_async_copy(qkv_bias_hbm, qkv_bias, load_sem.at[9]),
        pltpu.make_async_copy(out_bias_hbm, out_bias, load_sem.at[10]),
        pltpu.make_async_copy(prompt_lens_hbm, prompt_lens, load_sem.at[11]),
        pltpu.make_async_copy(suffix_lens_hbm, suffix_lens, load_sem.at[12]),
        pltpu.make_async_copy(group_sizes_hbm, group_sizes, load_sem.at[13]),
        pltpu.make_async_copy(choice_hbm, choice, load_sem.at[14]),
        pltpu.make_async_copy(chosen_hbm, chosen, load_sem.at[15]),
    ]
    for load in loads[6:] + loads[:6]:
        load.start()

    barrier = pltpu.get_barrier_semaphore()

    def greet(row, col):
        pl.semaphore_signal(
            barrier, inc=1, device_id=(row, col), device_id_type=pl.DeviceIdType.MESH
        )

    greet(r, sib)
    for step in range(1, rows):
        greet((r + step) % rows, c)

    @pl.when(z > 0)
    def _():
        greet(r, c - 2)

    @pl.when(z < planes - 1)
    def _():
        greet(r, c + 2)

    before = (z + planes - 1) // planes
    after = (2 * planes - 2 - z) // planes
    pl.semaphore_wait(barrier, rows + before + after)

    loads[6].wait()
    wide = hidden[...].astype(F32)
    width = wide.shape[1]
    own_mean = jnp.mean(wide, axis=1, keepdims=True)
    centred = wide - own_mean
    own_spread = jnp.sum(centred * centred, axis=1, keepdims=True)
    lane = lax.broadcasted_iota(jnp.int32, (block, 128), 1)
    stats[r] = jnp.where(lane == 0, own_mean, own_spread)

    def stat_copy(row):
        return to(stats.at[r], stats.at[r], stat_send.at[row], stat_recv.at[r], row, c)

    for step in range(1, rows):
        stat_copy((r + step) % rows).start()
    for step in range(1, rows):
        peer = (r + step) % rows
        to(stats.at[peer], stats.at[peer], stat_send.at[peer], stat_recv.at[peer], r, c).wait_recv()
    means = [stats[i][:, 0:1] for i in range(rows)]
    average = sum(means) / rows
    spread = sum(stats[i][:, 1:2] for i in range(rows))
    spread = spread + width * sum((m - average) * (m - average) for m in means)
    spread = spread / (width * rows)

    loads[7].wait()
    loads[8].wait()

    def x_rows(index):
        return pl.ds(pl.multiple_of(index * block, 16), block)

    x[x_rows(c), :] = (
        (hidden[...].astype(F32) - average)
        * lax.rsqrt(spread + 1e-05)
        * gain[...].astype(F32)[None]
        + shift[...].astype(F32)[None]
    ).astype(BF)

    def x_copy(way, group, col):
        at = x_rows(2 * group + k)
        return to(
            x.at[at], x.at[at], x_send.at[way, group], x_recv.at[2 * group + k], r, col
        )

    def x_wait(index):
        at = x_rows(index)
        to(x.at[at], x.at[at], x_send.at[0, 0], x_recv.at[index], r, c).wait_recv()

    def part_copy(group, row):
        return to(
            part_out.at[group, row],
            part_in.at[group, r],
            part_send.at[group, row],
            part_recv.at[group, r],
            row,
            c,
        )

    def low_copy(group, row):
        return to(
            low_own.at[group],
            low_in.at[group, r],
            low_send.at[group, row],
            low_recv.at[group, r],
            row,
            c,
        )

    def adapter(group):
        return chosen[choice[group]]

    def token_rows(group):
        return pl.ds(pl.multiple_of(group * GCAP, 16), GCAP)

    def project(group):
        low_own[group] = lax.dot_general(
            down_qkv[adapter(group)],
            x[token_rows(group), :],
            (((1,), (1,)), ((), ())),
            preferred_element_type=F32,
        )
        for step in range(1, rows):
            low_copy(group, (r + step) % rows).start()

        def one(step, _):
            row = (r + step) % rows
            cols = pl.ds(pl.multiple_of(row * HIDDEN_PART, 128), HIDDEN_PART)
            part = jnp.dot(
                x[token_rows(group), :], qkv_w[:, cols], preferred_element_type=F32
            )

            @pl.when(row != r)
            def _():
                part_out[group, row] = part.astype(BF)
                part_copy(group, row).start()

            @pl.when(row == r)
            def _():
                part_own[group] = part

            return 0

        lax.fori_loop(1, rows + 1, one, 0)

    def layout(group, axis):
        shape = (GCAP, 1) if axis == 0 else (1, GCAP)
        offsets = lax.broadcasted_iota(jnp.int32, shape, axis)
        prompt = prompt_lens[group]
        count = group_sizes[group]
        end = prompt
        request = jnp.zeros(shape, jnp.int32)
        begin = jnp.zeros(shape, jnp.int32)
        for j in range(suffix_lens.shape[1]):
            start = end
            end = end + jnp.where(j < count, suffix_lens[group, j], 0)
            passed = jnp.where(offsets >= end, 1, 0)
            begin = begin + jnp.where(offsets >= start, (1 - passed) * start, 0)
            request = request + passed
        inside = offsets < prompt
        position = jnp.where(inside, offsets, prompt + offsets - begin)
        request = jnp.where(inside, -1, jnp.where(request < count, request, -2))
        return offsets, request, position

    def allowed_of(group):
        _, request_q, position_q = layout(group, 0)
        key, request_k, position_k = layout(group, 1)
        square = (GCAP, GCAP)
        rq = jnp.broadcast_to(request_q, square)
        rk = jnp.broadcast_to(request_k, square)
        pq = jnp.broadcast_to(position_q, square)
        pk = jnp.broadcast_to(position_k, square)
        keys = jnp.broadcast_to(key, square)
        shared = (rk == -1) | ((rk == rq) & (rk != -2))
        near = (pq - pk < WIN) | (pk == 0)
        live = shared & (pk <= pq) & near & (rq != -2)
        return live | ((rq == -2) & (keys == 0))

    def mixed_copy(group, row_from):
        return to(
            mixed_out.at[group],
            mixed.at[group, k, pl.ds(0, GCAP), pl.ds(pl.multiple_of(row_from * 128, 128), 128)],
            mixed_send.at[group],
            mixed_recv.at[group, row_from],
            z,
            c,
        )

    def attend(group):
        low = low_own[group]
        proj = part_own[group] + own_bias[...]
        for step in range(1, rows):
            peer = (r + step) % rows
            to(
                low_own.at[group], low_in.at[group, peer],
                low_send.at[group, peer], low_recv.at[group, peer], r, c,
            ).wait_recv()
            low = low + low_in[group, peer]
        for step in range(1, rows):
            peer = (r + step) % rows
            to(
                part_out.at[group, peer], part_in.at[group, peer],
                part_send.at[group, peer], part_recv.at[group, peer], r, c,
            ).wait_recv()
            proj = proj + part_in[group, peer].astype(F32)
        proj = proj + lax.dot_general(
            low.astype(BF), up_qkv[adapter(group)], (((0,), (0,)), ((), ())),
            preferred_element_type=F32,
        )
        query = (proj[:, :HEAD_SIZE] * HEAD_SIZE ** (-0.5)).astype(BF)
        key = proj[:, HEAD_SIZE : 2 * HEAD_SIZE].astype(BF)
        value = proj[:, 2 * HEAD_SIZE :].astype(BF)
        allowed = allowed_of(group)
        scores = lax.dot_general(
            query, key, (((1,), (1,)), ((), ())), preferred_element_type=F32
        )
        scores = jnp.where(allowed, scores, -1e30)
        highest = jnp.max(scores, axis=1, keepdims=True)
        weights = jnp.where(allowed, jnp.exp(scores - highest), 0.0)
        probs = (weights / jnp.sum(weights, axis=1, keepdims=True)).astype(BF)
        rows_mixed = jnp.dot(probs, value, preferred_element_type=F32).astype(BF)

        @pl.when(r == z)
        def _():
            mixed[group, k, pl.ds(0, GCAP), pl.ds(pl.multiple_of(r * 128, 128), 128)] = rows_mixed
            mixed[group, k, pl.ds(GCAP, 16), :] = down_out[adapter(group)]

        @pl.when(r != z)
        def _():
            mixed_out[group] = rows_mixed
            mixed_copy(group, r).start()

    for load in loads[9:]:
        load.wait()

    parts = chain_recv.shape[2]
    part_width = mixed.shape[3] // parts

    def chain_at(group, half, part):
        return mixed.at[group, half, :, pl.ds(part * part_width, part_width)]

    def chain_copy(way, group, part, col):
        return to(
            chain_at(group, k, part), chain_at(group, k, part),
            chain_send.at[way, group, part], chain_recv.at[group, k, part], r, col,
        )

    def chain_wait(group, half, part):
        to(
            chain_at(group, half, part), chain_at(group, half, part),
            chain_send.at[0, group, part], chain_recv.at[group, half, part], r, c,
        ).wait_recv()

    def res_copy(group):
        return to(res_out.at[group], res_in.at[r], res_send.at[group], res_recv.at[r], group, c)

    def lowo_copy(group):
        return to(
            lowo_out.at[group], lowo_in.at[r], lowo_send.at[group], lowo_recv.at[r], group, c
        )

    half_rows = out_w.shape[0] // 2

    def combine(group):
        @pl.when(z == r)
        def _():
            for step in range(1, rows):
                mixed_copy(group, (r + step) % rows).wait_recv()

        for part in range(parts):
            @pl.when(z != r)
            def _():
                chain_wait(group, k, part)

            @pl.when((z >= r) & (z < planes - 1))
            def _():
                chain_copy(0, group, part, c + 2).start()

            @pl.when((z <= r) & (z > 0))
            def _():
                chain_copy(1, group, part, c - 2).start()

            chain_copy(2, group, part, sib).start()
        for part in range(parts):
            chain_wait(group, 1 - k, part)
        low = jnp.zeros((16, GCAP), F32)
        part = jnp.zeros((GCAP, out_w.shape[1]), F32)
        for half in range(2):
            tokens = mixed[group, half, pl.ds(0, GCAP), :]
            low = low + lax.dot_general(
                mixed[group, half, pl.ds(GCAP, 16), :], tokens, (((1,), (1,)), ((), ())),
                preferred_element_type=F32,
            )
            part = part + jnp.dot(
                tokens, out_w[half * half_rows : (half + 1) * half_rows, :],
                preferred_element_type=F32,
            )

        @pl.when(group != r)
        def _():
            lowo_out[group] = low
            lowo_copy(group).start()
            res_out[group] = part.astype(BF)
            res_copy(group).start()

        @pl.when(group == r)
        def _():
            lowo_own[...] = low
            res_own[...] = part

    bias = qkv_bias[...].astype(F32)[None]
    own_bias[...] = sum(
        jnp.where(r == head, bias[:, head * HIDDEN_PART : (head + 1) * HIDDEN_PART], 0.0)
        for head in range(rows)
    )

    def first(step, _):
        @pl.when(step < planes)
        def _():
            for side in range(2):
                group = z + step * (2 * side - 1)
                valid = (group >= 0) & (group < planes)
                if side == 1:
                    valid = valid & (step > 0)

                @pl.when(valid)
                def _():
                    @pl.when(step > 0)
                    def _():
                        x_wait(2 * group + k)

                    @pl.when((group <= z) & (z < planes - 1))
                    def _():
                        x_copy(0, group, c + 2).start()

                    @pl.when((group >= z) & (z > 0))
                    def _():
                        x_copy(1, group, c - 2).start()

                    x_copy(2, group, sib).start()

            @pl.when(step == 0)
            def _():
                loads[0].wait()
                loads[1].wait()

            def compute(side, _):
                group = z + step * (2 * side - 1)

                @pl.when((group >= 0) & (group < planes) & (step + 1 - side > 0))
                def _():
                    x_wait(2 * group + 1 - k)
                    project(group)

                return 0

            lax.fori_loop(0, 2, compute, 0)

        @pl.when((step > 0) & (step <= planes))
        def _():
            @pl.when(step == 1)
            def _():
                for load in loads[2:6]:
                    load.wait()

            def mix(side, _):
                group = z + (step - 1) * (2 * side - 1)

                @pl.when((group >= 0) & (group < planes) & (step - side > 0))
                def _():
                    attend(group)

                return 0

            lax.fori_loop(0, 2, mix, 0)

        away = ((r - z) * (r - z) + planes * planes - 1) // (planes * planes)
        behind = step - 2 - away * (planes - 1)

        @pl.when((behind >= 0) & (behind < planes))
        def _():
            def join(side, _):
                group = r + behind * (2 * side - 1)

                @pl.when((group >= 0) & (group < planes) & (behind + 1 - side > 0))
                def _():
                    combine(group)

                return 0

            lax.fori_loop(0, 2, join, 0)

        return 0

    lax.fori_loop(0, 2 * planes + 1, first, 0)

    _, request, _ = layout(r, 0)
    alive = jnp.where(request != -2, 1.0, 0.0)
    low = lowo_own[...]
    total = res_own[...] + out_bias[...].astype(F32)[None]
    for step in range(1, rows):
        peer = (r + step) % rows
        to(
            lowo_out.at[peer], lowo_in.at[peer], lowo_send.at[peer], lowo_recv.at[peer], r, c
        ).wait_recv()
        low = low + lowo_in[peer]
    for step in range(1, rows):
        peer = (r + step) % rows
        to(
            res_out.at[peer], res_in.at[peer], res_send.at[peer], res_recv.at[peer], r, c
        ).wait_recv()
        total = total + res_in[peer].astype(F32)
    total = total + lax.dot_general(
        low.astype(BF), up_out[adapter(r)], (((0,), (0,)), ((), ())), preferred_element_type=F32
    )
    out[...] = (total * alive).astype(BF)

    for step in range(1, rows):
        peer = (r + step) % rows
        stat_copy(peer).wait_send()
        res_copy(peer).wait_send()
        lowo_copy(peer).wait_send()

    def drain(group, _):
        @pl.when((group <= z) & (z < planes - 1))
        def _():
            x_copy(0, group, c + 2).wait_send()

        @pl.when((group >= z) & (z > 0))
        def _():
            x_copy(1, group, c - 2).wait_send()

        x_copy(2, group, sib).wait_send()
        for step in range(1, rows):
            peer = (r + step) % rows
            low_copy(group, peer).wait_send()
            part_copy(group, peer).wait_send()

        @pl.when(r != z)
        def _():
            mixed_copy(group, r).wait_send()

        for part in range(parts):
            @pl.when((z >= r) & (z < planes - 1))
            def _():
                chain_copy(0, group, part, c + 2).wait_send()

            @pl.when((z <= r) & (z > 0))
            def _():
                chain_copy(1, group, part, c - 2).wait_send()

            chain_copy(2, group, part, sib).wait_send()
        return 0

    lax.fori_loop(0, planes, drain, 0)


def fused(
    hidden,
    ln_gain,
    ln_shift,
    qkv_weight,
    qkv_bias,
    out_weight,
    out_bias,
    down_qkv,
    up_qkv,
    down_out,
    up_out,
    prompt_lens,
    suffix_lens,
    group_sizes,
    group_adapter_choice,
    chosen,
):
    groups = lax.axis_size("row")
    block, width = hidden.shape
    out_cols = out_weight.shape[1]
    bank, rank = down_out.shape[0], down_out.shape[1]
    down_t = jnp.transpose(down_qkv, (0, 2, 1))
    vmem = pl.BlockSpec(memory_space=pltpu.VMEM)
    hbm = pl.BlockSpec(memory_space=pl.ANY)
    dma = pltpu.SemaphoreType.DMA
    half = HEAD_SIZE * groups
    macs = groups * GCAP * (qkv_weight.size + out_weight.size)
    return pl.pallas_call(
        functools.partial(fused_kernel, groups),
        out_shape=jax.ShapeDtypeStruct((GCAP, out_cols), BF),
        in_specs=[hbm] * 16,
        out_specs=vmem,
        scratch_shapes=[
            pltpu.VMEM(hidden.shape, BF),
            pltpu.VMEM(ln_gain.shape, BF),
            pltpu.VMEM(ln_shift.shape, BF),
            pltpu.VMEM(qkv_bias.shape, BF),
            pltpu.VMEM(out_bias.shape, BF),
            pltpu.SMEM(prompt_lens.shape, jnp.int32),
            pltpu.SMEM(suffix_lens.shape, jnp.int32),
            pltpu.SMEM(group_sizes.shape, jnp.int32),
            pltpu.SMEM(group_adapter_choice.shape, jnp.int32),
            pltpu.SMEM(chosen.shape, jnp.int32),
            pltpu.VMEM(qkv_weight.shape, BF),
            pltpu.VMEM(out_weight.shape, BF),
            pltpu.VMEM(down_t.shape, BF),
            pltpu.VMEM((bank, rank, HIDDEN_PART), BF),
            pltpu.VMEM(down_out.shape, BF),
            pltpu.VMEM(up_out.shape, BF),
            pltpu.VMEM((groups, block, 128), F32),
            pltpu.VMEM((groups * GCAP, width), BF),
            pltpu.VMEM((groups, groups, GCAP, HIDDEN_PART), BF),
            pltpu.VMEM((groups, groups, GCAP, HIDDEN_PART), BF),
            pltpu.VMEM((groups, GCAP, HIDDEN_PART), F32),
            pltpu.VMEM((groups, rank, GCAP), F32),
            pltpu.VMEM((groups, groups, rank, GCAP), F32),
            pltpu.VMEM((groups, GCAP, HEAD_SIZE), BF),
            pltpu.VMEM((groups, 2, GCAP + rank, half), BF),
            pltpu.VMEM((groups, GCAP, out_cols), BF),
            pltpu.VMEM((groups, GCAP, out_cols), BF),
            pltpu.VMEM((GCAP, out_cols), F32),
            pltpu.VMEM((groups, rank, GCAP), F32),
            pltpu.VMEM((groups, rank, GCAP), F32),
            pltpu.VMEM((rank, GCAP), F32),
            pltpu.VMEM((1, HIDDEN_PART), F32),
            dma((16,)),
            dma((groups,)),
            dma((groups,)),
            dma((3, groups)),
            dma((2 * groups,)),
            dma((groups, groups)),
            dma((groups, groups)),
            dma((groups, groups)),
            dma((groups, groups)),
            dma((groups,)),
            dma((groups, groups)),
            dma((3, groups, 2)),
            dma((groups, 2, 2)),
            dma((groups,)),
            dma((groups,)),
            dma((groups,)),
            dma((groups,)),
        ],
        compiler_params=pltpu.CompilerParams(
            collective_id=0, has_side_effects=True, vmem_limit_bytes=60 * 2**20
        ),
        cost_estimate=pl.CostEstimate(
            flops=2 * macs, bytes_accessed=2 * (qkv_weight.size + out_weight.size), transcendentals=0
        ),
    )(
        hidden,
        ln_gain,
        ln_shift,
        qkv_bias,
        out_bias,
        prompt_lens,
        suffix_lens,
        group_sizes,
        group_adapter_choice,
        chosen,
        qkv_weight,
        out_weight,
        down_t,
        up_qkv,
        down_out,
        up_out,
    )


def block_of(*arrays):
    groups = lax.axis_size("row")
    heads_here = arrays[4].shape[0] // HIDDEN_PART
    if heads_here == groups and lax.axis_size("col") == 2 * groups and arrays[5].shape[1] % 128 == 0:
        return fused(*arrays)
    return local(*arrays)


def solution(mesh):
    in_specs = (
        P("col", "row"),
        P("row"),
        P("row"),
        P("row", "col"),
        P("col"),
        P("row", "col"),
        P("col"),
        P(None, "row", None),
        P(None, None, "col"),
        P(None, None, "col"),
        P(None, None, "col"),
        P(),
        P(),
        P(),
        P(),
        P(),
    )
    out_specs = P("row", "col")
    return jax.shard_map(block_of, mesh=mesh, in_specs=in_specs, out_specs=out_specs, check_vma=False)
```
